256 devices in a mesh: probe: 8 (over y, x_hi), tm: 16 (over x_lo, z), lane: 2 (over core).
Axes of the slice: x: 4 (x_hi: 2, x_lo: 2; x = x_hi * 2 + x_lo), y: 4, z: 8, core: 2. Of those that a mesh axis runs over, the one named last changes fastest.
Arguments:
- volt: bfloat16 [8, 2, 4096, 480], P('probe', 'lane', 'tm'), may hold values from -40 to 40
- keep: int32 [8, 2, 4096], P('probe', 'lane', 'tm'), may hold values 0 or 1
- site_ids: int32 [8, 2], P('probe', 'lane'), may hold values from 0 to 59
- probe_ids: int32 [8], P('probe'), may hold values from 0 to 7, each once
- w_patch: bfloat16 [480, 768], replicated, may hold values from -0.25 to 0.25
- site_table: bfloat16 [60, 768], replicated, may hold values from -3 to 3
- probe_table: bfloat16 [8, 768], replicated, may hold values from -3 to 3
- mask_token: bfloat16 [768], replicated, may hold values from -3 to 3
- gain_time: bfloat16 [768], replicated, may hold values from 0.099609375 to 1.8984375
- w_qkv_time: bfloat16 [768, 2304], replicated, may hold values from -6 to 6
- w_out_time: bfloat16 [768, 768], replicated, may hold values from -0.21875 to 0.21875
- gain_cross: bfloat16 [768], replicated, may hold values from 0.099609375 to 1.8984375
- w_qkv_cross: bfloat16 [768, 2304], replicated, may hold values from -6 to 6
- w_out_cross: bfloat16 [768, 768], replicated, may hold values from -0.21875 to 0.21875
Outputs:
- encoded: bfloat16 [8, 2, 4096, 768], P('probe', 'lane', 'tm')
The draws below stay inside these ranges and needn't reach their ends.
All inputs are finite; a program needn't handle non-finite values. No bound on the sum of `keep` on one device may be relied on, other than what follows from the above.
Results may differ from the reference program's by a relative error of at most 0.024.
Values may be sent and summed in bfloat16 or wider, within the bound.
No kernel may reach another device: no remote copies, remote signals or barrier semaphores. Data moves between devices by JAX's collectives and lax.ppermute only.
A program may use at most 192 MiB of HBM per device.

```python
import math
import jax
import jax.numpy as jnp
from jax import lax

HEADS = 12
HEAD_DIM = 64
D = 768
PATCH = 480
SITE_ROWS = 60
WIN = 16
PROBES = 8
SITES = 2
TIMES = 4096


def draw_volt(key, part):
    first = jax.random.fold_in(key, 0)
    shape = (PROBES, SITES, TIMES, PATCH)
    fresh = jax.random.normal(first, shape, jnp.float32)
    return jnp.clip(fresh, -6.0, 6.0).astype(jnp.bfloat16)


def projection_draw(key):
    first = jax.random.fold_in(key, 0)
    base = jax.random.normal(first, (D, 3 * D), jnp.float32)
    sharp = 1.7 / math.sqrt(D)
    queries = base[:, :D] * sharp
    keys = base[:, D:2 * D] * sharp
    values = base[:, 2 * D:] / math.sqrt(D)
    return jnp.clip(jnp.concatenate([queries, keys, values], axis=1), -6.0, 6.0)


def draw_w_qkv_time(key, part):
    return projection_draw(jax.random.fold_in(key, 3)).astype(jnp.bfloat16)


def draw_w_qkv_cross(key, part):
    return projection_draw(jax.random.fold_in(key, 7)).astype(jnp.bfloat16)


def with_ends(values, key, smallest, largest):
    longest = values.shape.index(max(values.shape))
    spots = []
    for shift in (0, 1):
        where = [jax.random.randint(jax.random.fold_in(key, axis), (), 0, length) for axis, length in enumerate(values.shape)]
        where[longest] = (where[longest] + shift) % values.shape[longest]
        spots.append(tuple(where))
    return values.at[spots[0]].set(smallest).at[spots[1]].set(largest)


def scatter_about(key, dims, scale, bound, kind=jnp.bfloat16):
    result = scale * jax.random.normal(key, dims, jnp.float32)
    return jnp.clip(result, min=-bound, max=bound).astype(kind)


def setup_inputs(seed: int = 0) -> dict:
    seeds = jax.random.split(jax.random.key(seed), 15)
    return {
        "volt": draw_volt(jax.random.fold_in(seeds[14], 71), 0),
        "keep": with_ends((jax.random.randint(seeds[1], (PROBES, SITES, TIMES), 0, 4) < 1).astype(jnp.int32), jax.random.fold_in(seeds[1], 1), 0, 1),
        "site_ids": with_ends(jax.random.randint(seeds[2], (PROBES, SITES), 0, SITE_ROWS), jax.random.fold_in(seeds[2], 1), 0, SITE_ROWS - 1).astype(jnp.int32),
        "probe_ids": jax.random.permutation(seeds[3], PROBES).astype(jnp.int32),
        "w_patch": scatter_about(seeds[4], (PATCH, D), PATCH ** -0.5, 0.25),
        "site_table": scatter_about(seeds[5], (SITE_ROWS, D), 0.5, 3.0),
        "probe_table": scatter_about(seeds[6], (PROBES, D), 0.5, 3.0),
        "mask_token": scatter_about(seeds[7], (D,), 0.5, 3.0),
        "gain_time": jnp.clip(1.0 + 0.18 * jax.random.normal(seeds[8], (D,), jnp.float32), 0.099609375, 1.8984375).astype(jnp.bfloat16),
        "w_qkv_time": draw_w_qkv_time(jax.random.fold_in(seeds[14], 71), 0),
        "w_out_time": scatter_about(seeds[10], (D, D), D ** -0.5, 0.21875),
        "gain_cross": jnp.clip(1.0 + 0.18 * jax.random.normal(seeds[11], (D,), jnp.float32), 0.099609375, 1.8984375).astype(jnp.bfloat16),
        "w_qkv_cross": draw_w_qkv_cross(jax.random.fold_in(seeds[14], 71), 0),
        "w_out_cross": scatter_about(seeds[13], (D, D), D ** -0.5, 0.21875),
    }


def time_code(times, width):
    half = width // 2
    freq = jnp.exp(jnp.arange(half, dtype=jnp.float32) * (-math.log(10000.0) / half))
    angle = times.astype(jnp.float32)[:, None] * freq[None, :]
    return jnp.concatenate([jnp.sin(angle), jnp.cos(angle)], axis=1)

def layer_norm(rows, gain):
    middle = lax.optimization_barrier(jnp.mean(rows, axis=-1, keepdims=True))
    centred = rows - middle
    spread = lax.optimization_barrier(jnp.mean(centred * centred, axis=-1, keepdims=True))
    return centred * lax.rsqrt(spread + 1e-05) * gain.astype(jnp.float32)

def lookup(ids, table):
    flat = ids.reshape(-1)
    onehot = (flat[:, None] == jnp.arange(table.shape[0], dtype=jnp.int32)[None, :]).astype(table.dtype)
    found = jnp.dot(onehot, table, preferred_element_type=jnp.float32)
    return found.reshape(ids.shape + (table.shape[1],))

def attend(queries, keys, values, allowed):
    scale = 1.0 / math.sqrt(HEAD_DIM)
    scores = jnp.einsum('qhc,khc->hqk', queries.astype(jnp.float32), keys.astype(jnp.float32)) * scale
    allowed = allowed[None, :, :]
    top = lax.optimization_barrier(jnp.max(jnp.where(allowed, scores, -1e+30), axis=-1, keepdims=True))
    weights = jnp.where(allowed, jnp.exp(scores - top), 0.0)
    total = lax.optimization_barrier(jnp.sum(weights, axis=-1))
    rounded = lax.optimization_barrier(weights.astype(jnp.bfloat16))
    mixed = jnp.einsum('hqk,khc->hqc', rounded.astype(jnp.float32), values.astype(jnp.float32))
    context = mixed / total[..., None]
    count = queries.shape[0]
    return jnp.transpose(context, (1, 0, 2)).reshape(count, HEADS * HEAD_DIM).astype(jnp.bfloat16)

def reference(volt, keep, site_ids, probe_ids, w_patch, site_table, probe_table, mask_token, gain_time, w_qkv_time, w_out_time, gain_cross, w_qkv_cross, w_out_cross):
    width = w_patch.shape[1]
    probes, sites, times, patch = volt.shape
    proj = jnp.dot(volt.reshape(-1, patch), w_patch, preferred_element_type=jnp.float32).reshape(probes, sites, times, width)
    proj = jnp.where((keep == 1)[..., None], proj, mask_token.astype(jnp.float32)[None, None, None, :])
    site_vec = lookup(site_ids, site_table)
    probe_vec = lookup(probe_ids, probe_table)
    code = time_code(jnp.arange(times, dtype=jnp.int32), width)
    x0 = (proj + site_vec[:, :, None, :] + probe_vec[:, None, None, :] + code[None, None]).astype(jnp.bfloat16)
    h1 = layer_norm(x0.astype(jnp.float32), gain_time).astype(jnp.bfloat16)
    qkv1 = jnp.dot(h1.reshape(-1, width), w_qkv_time, preferred_element_type=jnp.float32).astype(jnp.bfloat16)
    qkv1 = qkv1.reshape(probes * sites, times, 3 * width)
    keep_seq = keep.reshape(probes * sites, times)
    block = math.gcd(times, 512)
    starts = jnp.arange(times // block, dtype=jnp.int32) * block
    key_pos = jnp.arange(times, dtype=jnp.int32)

    def temporal(pair):
        seq, visible = pair
        queries = seq[:, :width].reshape(times, HEADS, HEAD_DIM)
        keys = seq[:, width:2 * width].reshape(times, HEADS, HEAD_DIM)
        values = seq[:, 2 * width:].reshape(times, HEADS, HEAD_DIM)

        def one_block(start):
            part = lax.dynamic_slice_in_dim(queries, start, block, 0)
            query_pos = start + jnp.arange(block, dtype=jnp.int32)
            allowed = (visible[None, :] == 1) | (query_pos[:, None] == key_pos[None, :])
            return attend(part, keys, values, allowed)
        return lax.map(one_block, starts).reshape(times, width)
    ctx1 = lax.map(temporal, (qkv1, keep_seq)).reshape(probes, sites, times, width)
    x1 = (x0.astype(jnp.float32) + jnp.dot(ctx1.reshape(-1, width), w_out_time, preferred_element_type=jnp.float32).reshape(probes, sites, times, width)).astype(jnp.bfloat16)
    h2 = layer_norm(x1.astype(jnp.float32), gain_cross).astype(jnp.bfloat16)
    qkv2 = jnp.dot(h2.reshape(-1, width), w_qkv_cross, preferred_element_type=jnp.float32).astype(jnp.bfloat16)
    nwin = times // WIN
    qkv2 = qkv2.reshape(probes, sites, nwin, WIN, 3 * width).transpose(2, 0, 1, 3, 4).reshape(nwin, probes * sites * WIN, 3 * width)
    keep_win = keep.reshape(probes, sites, nwin, WIN).transpose(2, 0, 1, 3).reshape(nwin, probes * sites * WIN)
    count = probes * sites * WIN
    same = jnp.arange(count, dtype=jnp.int32)

    def cross(pair):
        rows, visible = pair
        queries = rows[:, :width].reshape(count, HEADS, HEAD_DIM)
        keys = rows[:, width:2 * width].reshape(count, HEADS, HEAD_DIM)
        values = rows[:, 2 * width:].reshape(count, HEADS, HEAD_DIM)
        allowed = (visible[None, :] == 1) | (same[:, None] == same[None, :])
        return attend(queries, keys, values, allowed)
    ctx2 = lax.map(cross, (qkv2, keep_win))
    ctx2 = ctx2.reshape(nwin, probes, sites, WIN, width).transpose(1, 2, 0, 3, 4).reshape(probes, sites, times, width)
    out = x1.astype(jnp.float32) + jnp.dot(ctx2.reshape(-1, width), w_out_cross, preferred_element_type=jnp.float32).reshape(probes, sites, times, width)
    return out.astype(jnp.bfloat16)
```

```python
import functools
import math

import jax
import jax.numpy as jnp
from jax import lax
from jax.experimental import pallas as pl
from jax.experimental.pallas import tpu as pltpu
from jax.sharding import PartitionSpec as P

HEADS = 12
HEAD_DIM = 64
WIN = 16
PAIRS = HEADS // 2
PACKED = 512
COL_TIME, COL_VALID, COL_COUNT = 480, 481, 482
CAP = 96
FAR = -1e30
BF = jnp.bfloat16
F32 = jnp.float32
VMEM_LIMIT = 60 * 1024 * 1024
NT = (((1,), (1,)), ((), ()))


def iota(shape, dim):
    return lax.broadcasted_iota(jnp.int32, shape, dim)


def mm(a, b):
    return jnp.dot(a, b, preferred_element_type=F32)


def norm(rows, gain):
    middle = jnp.mean(rows, axis=-1, keepdims=True)
    centred = rows - middle
    spread = jnp.mean(centred * centred, axis=-1, keepdims=True)
    return centred * lax.rsqrt(spread + 1e-05) * gain


def split(value):
    high = value.astype(BF)
    return high, (value - high.astype(F32)).astype(BF)


def to_column(row):
    n = row.shape[1]
    eye = iota((n, n), 0) == iota((n, n), 1)
    return jnp.sum(jnp.where(eye, row, 0.0), axis=1, keepdims=True)


def call(kernel, out, args, *, smem=(), any_space=(), smem_out=(), scratch=(), flops=0, nbytes=0):
    specs = []
    for i in range(len(args)):
        space = pltpu.SMEM if i in smem else pl.ANY if i in any_space else pltpu.VMEM
        specs.append(pl.BlockSpec(memory_space=space))
    outs = [
        pl.BlockSpec(memory_space=pltpu.SMEM if i in smem_out else pltpu.VMEM)
        for i in range(len(jax.tree.leaves(out)))
    ]
    return pl.pallas_call(
        kernel,
        out_shape=out,
        in_specs=specs,
        out_specs=outs if isinstance(out, tuple) else outs[0],
        scratch_shapes=list(scratch),
        compiler_params=pltpu.CompilerParams(vmem_limit_bytes=VMEM_LIMIT),
        cost_estimate=pl.CostEstimate(flops=flops, bytes_accessed=nbytes, transcendentals=0),
    )(*args)


def pack_kernel(keep_ref, volt_ref, out_ref, wide):
    count, samples = volt_ref.shape
    cap = out_ref.shape[0]
    lane = iota((count, PACKED), 1)
    extra = jnp.where(
        lane == COL_TIME, iota((count, PACKED), 0).astype(F32), jnp.where(lane == COL_VALID, 1.0, 0.0)
    )
    wide[...] = extra.astype(BF)
    wide[:, :samples] = volt_ref[...]
    mask = keep_ref[...].astype(F32)
    upper = jnp.where(iota((count, count), 0) <= iota((count, count), 1), 1.0, 0.0).astype(BF)
    rank = mm(jnp.broadcast_to(mask, (16, count)).astype(BF), upper)[0:1, :]
    pick = (rank - 1.0 == iota((cap, count), 0).astype(F32)) & (mask > 0.5)
    packed = mm(jnp.where(pick, 1.0, 0.0).astype(BF), wide[...])
    total = jnp.sum(mask, axis=1, keepdims=True)
    out_ref[...] = jnp.where(iota(packed.shape, 1) == COL_COUNT, total, packed).astype(BF)


def frequencies(rows, half):
    return jnp.exp(iota((rows, half), 1).astype(F32) * (-math.log(10000.0) / half))


def own_kernel(
    ids_ref,
    keep_ref,
    volt_ref,
    w_patch_ref,
    site_ref,
    probe_ref,
    token_ref,
    gain_ref,
    w_qkv_ref,
    x0_ref,
    q_ref,
    self_ref,
    v_ref,
    tab_ref,
    big_ref,
    base_ref,
):
    count, width = x0_ref.shape
    half = width // 2
    steps = big_ref.shape[0]
    fine = iota((count, half), 0).astype(F32) * frequencies(count, half)
    sin_l, cos_l = jnp.sin(fine), jnp.cos(fine)
    coarse = (iota((steps, half), 0) * count).astype(F32) * frequencies(steps, half)
    big_ref[:, :half] = jnp.sin(coarse)
    big_ref[:, half:] = jnp.cos(coarse)
    for at, value in ((0, sin_l), (half, cos_l)):
        high, low = split(value)
        tab_ref[:, at : at + half] = high
        tab_ref[:, width + at : width + at + half] = low
    me = ids_ref[2]
    row = big_ref[pl.ds(me, 1), :]
    sin_d, cos_d = row[:, :half], row[:, half:]
    code = jnp.concatenate([sin_d * cos_l + cos_d * sin_l, cos_d * cos_l - sin_d * sin_l], axis=1)

    sites, probes = site_ref.shape[0], probe_ref.shape[0]
    one_site = jnp.where(iota((16, sites), 1) == ids_ref[0], 1.0, 0.0).astype(BF)
    one_probe = jnp.where(iota((16, probes), 1) == ids_ref[1], 1.0, 0.0).astype(BF)
    base = mm(one_site, site_ref[...])[0:8] + mm(one_probe, probe_ref[...])[0:8]
    base_ref[...] = base

    keep = to_column(keep_ref[...].astype(F32))
    proj = mm(volt_ref[...], w_patch_ref[...])
    proj = jnp.where(keep > 0.5, proj, token_ref[...].astype(F32))
    x0 = (proj + base[0:1] + code).astype(BF)
    x0_ref[...] = x0
    h1 = norm(x0.astype(F32), gain_ref[...].astype(F32)).astype(BF)
    qkv = mm(h1, w_qkv_ref[...]).astype(BF)
    queries = (qkv[:, :width].astype(F32) * (1.0 / math.sqrt(HEAD_DIM))).astype(BF)
    q_ref[...] = queries
    v_ref[...] = qkv[:, 2 * width :]
    product = queries.astype(F32) * qkv[:, width : 2 * width].astype(F32)
    same_head = jnp.where(iota((128, 128), 0) // HEAD_DIM == iota((128, 128), 1) // HEAD_DIM, 1.0, 0.0).astype(BF)
    for pair in range(PAIRS):
        cols = slice(pair * 128, pair * 128 + 128)
        high, low = split(product[:, cols])
        score = mm(high, same_head) + mm(low, same_head)
        self_ref[:, cols] = jnp.where(keep > 0.5, FAR, score)


def time_kernel(
    sources,
    cap,
    nblocks,
    src_ref,
    keep_ref,
    w_patch_ref,
    tab_ref,
    big_ref,
    base_ref,
    gain_ref,
    w_qkv_ref,
    q_ref,
    self_ref,
    v_ref,
    x0_ref,
    w_out_ref,
    *rest,
):
    blocks = rest[:nblocks]
    out_ref, over_ref, kx, vx, ctx = rest[nblocks:]
    count, width = x0_ref.shape
    half = width // 2
    samples = w_patch_ref.shape[0]
    gain = gain_ref[...].astype(F32)
    base = base_ref[0:1, :]
    most = jnp.zeros((1, 1), F32)
    slot = 0
    for block, parts in zip(blocks, sources):
        for part in range(parts):
            rows = block[part * cap : (part + 1) * cap, :]
            tail = rows[:, 384:512].astype(F32)
            local = tail[:, COL_TIME - 384 : COL_TIME - 383]
            valid = tail[:, COL_VALID - 384 : COL_VALID - 383]
            most = jnp.maximum(most, tail[0:1, COL_COUNT - 384 : COL_COUNT - 383])
            proj = mm(rows[:, :samples], w_patch_ref[...])
            pick = jnp.where(iota((cap, count), 1).astype(F32) == local, 1.0, 0.0).astype(BF)
            found = mm(pick, tab_ref[...])
            found = found[:, :width] + found[:, width:]
            sin_l, cos_l = found[:, :half], found[:, half:]
            row = big_ref[pl.ds(src_ref[slot], 1), :]
            sin_d, cos_d = row[:, :half], row[:, half:]
            code = jnp.concatenate(
                [sin_d * cos_l + cos_d * sin_l, cos_d * cos_l - sin_d * sin_l], axis=1
            )
            x0 = (proj + base + code).astype(BF)
            h1 = norm(x0.astype(F32), gain).astype(BF)
            kv = mm(h1, w_qkv_ref[:, width:]).astype(BF)
            lane = iota((cap, 128), 1)
            bias = jnp.where((lane == 0) & (valid < 0.5), FAR, 0.0).astype(BF)
            ones = jnp.ones((cap, 128), BF)
            at = slice(slot * cap, (slot + 1) * cap)
            for pair in range(PAIRS):
                kx[pair, at, :128] = kv[:, pair * 128 : pair * 128 + 128]
                kx[pair, at, 128:] = bias
                vx[pair, at, :128] = kv[:, width + pair * 128 : width + pair * 128 + 128]
                vx[pair, at, 128:] = ones
            slot += 1
    over_ref[0, 0] = jnp.max(most).astype(jnp.int32)

    lane = iota((count, 128), 1)
    low = lane < HEAD_DIM
    mark = jnp.where(lane == 0, 1.0, 0.0).astype(BF)

    def one_pair(pair, carry):
        cols = pl.ds(pl.multiple_of(pair * 128, 128), 128)
        queries = q_ref[:, cols]
        zero = jnp.zeros_like(queries)
        both = jnp.concatenate(
            [
                jnp.concatenate([jnp.where(low, queries, zero), mark], axis=1),
                jnp.concatenate([jnp.where(low, zero, queries), mark], axis=1),
            ],
            axis=0,
        )
        scores = lax.dot_general(both, kx[pair], NT, preferred_element_type=F32)
        own = self_ref[:, cols]
        own = jnp.concatenate([own[:, 0:1], own[:, HEAD_DIM : HEAD_DIM + 1]], axis=0)
        top = jnp.maximum(jnp.max(scores, axis=1, keepdims=True), own)
        weights = jnp.exp(scores - top).astype(BF)
        mixed = mm(weights, vx[pair])
        own = jnp.exp(own - top)
        total = mixed[:, 128:] + own
        own = own.astype(BF).astype(F32)
        values = v_ref[:, cols].astype(F32)
        first = (mixed[:count, :128] + own[:count] * values) / total[:count]
        second = (mixed[count:, :128] + own[count:] * values) / total[count:]
        ctx[:, cols] = jnp.where(low, first, second).astype(BF)
        return carry

    lax.fori_loop(0, PAIRS, one_pair, 0)
    x1 = x0_ref[...].astype(F32) + mm(ctx[...], w_out_ref[...])
    out_ref[:, :width] = x1.astype(BF)
    keep = to_column(keep_ref[...].astype(F32))
    out_ref[:, width:] = jnp.broadcast_to(keep, (count, 128)).astype(BF)


def cross_kernel(x_ref, gain_ref, w_qkv_ref, w_out_ref, out_ref, ctx):
    count, width = out_ref.shape
    x1 = x_ref[:, :width].astype(F32)
    h2 = norm(x1, gain_ref[...].astype(F32)).astype(BF)
    qkv = mm(h2, w_qkv_ref[...]).astype(BF)
    seen = x_ref[:, width:].astype(F32)[:, 0:1]
    eye = iota((count, count), 0) == iota((count, count), 1)
    seen = jnp.sum(jnp.where(eye, seen, 0.0), axis=0, keepdims=True)
    bias = jnp.where(eye | (seen > 0.5), 0.0, FAR)
    bias = jnp.concatenate([bias, bias], axis=0)
    lane = iota((count, 128), 1)
    low = lane < HEAD_DIM
    scale = 1.0 / math.sqrt(HEAD_DIM)
    ones = jnp.ones((count, 128), BF)
    for pair in range(PAIRS):
        at = pair * 128
        queries = (qkv[:, at : at + 128].astype(F32) * scale).astype(BF)
        zero = jnp.zeros_like(queries)
        both = jnp.concatenate([jnp.where(low, queries, zero), jnp.where(low, zero, queries)], axis=0)
        scores = lax.dot_general(both, qkv[:, width + at : width + at + 128], NT, preferred_element_type=F32)
        scores = scores + bias
        top = jnp.max(scores, axis=1, keepdims=True)
        weights = jnp.exp(scores - top).astype(BF)
        values = jnp.concatenate([qkv[:, 2 * width + at : 2 * width + at + 128], ones], axis=1)
        mixed = mm(weights, values)
        done = mixed[:, :128] / mixed[:, 128:]
        ctx[:, at : at + 128] = jnp.where(low, done[:count], done[count:]).astype(BF)
    out_ref[...] = (x1 + mm(ctx[...], w_out_ref[...])).astype(BF)


def body(
    volt,
    keep,
    site_ids,
    probe_ids,
    w_patch,
    site_table,
    probe_table,
    mask_token,
    gain_time,
    w_qkv_time,
    w_out_time,
    gain_cross,
    w_qkv_cross,
    w_out_cross,
):
    width = w_patch.shape[1]
    rows = volt[0, 0]
    count = rows.shape[0]
    mask = keep[0]
    me = lax.axis_index("tm")
    nx, nz = 2, 8
    steps = nx * nz

    def shift(array, dx, dz):
        pairs = []
        for i in range(steps):
            x, z = divmod(i, nz)
            pairs.append((i, ((x + dx) % nx) * nz + (z + dz) % nz))
        return lax.ppermute(array, "tm", pairs)

    def pack(cap):
        return call(
            pack_kernel,
            jax.ShapeDtypeStruct((cap, PACKED), BF),
            (mask, rows),
            scratch=(pltpu.VMEM((count, PACKED), BF),),
            flops=2 * cap * count * PACKED,
            nbytes=500_000,
        )

    def gather(own, cap):
        below, above, beside = shift(own, 0, 1), shift(own, 0, -1), shift(own, 1, 0)
        down2 = shift(jnp.concatenate([below, beside], axis=0), 0, 1)
        up2 = shift(jnp.concatenate([above, beside], axis=0), 0, -1)
        down3, up3 = shift(down2, 0, 1), shift(up2, 0, -1)
        down4 = shift(down3, 0, 1)
        up4 = shift(up3[cap:], 0, -1)
        far = shift(up3[:cap], 1, -1)
        return (
            (own, [(0, 0)]),
            (below, [(0, -1)]),
            (above, [(0, 1)]),
            (beside, [(1, 0)]),
            (down2, [(0, -2), (1, -1)]),
            (up2, [(0, 2), (1, 1)]),
            (down3, [(0, -3), (1, -2)]),
            (up3, [(0, 3), (1, 2)]),
            (down4, [(0, -4), (1, -3)]),
            (up4, [(1, 3)]),
            (far, [(1, 4)]),
        )

    packed = pack(CAP)
    ids = jnp.stack([site_ids[0, 0], probe_ids[0], me.astype(jnp.int32)])
    row = lambda v: v.reshape(1, width)
    x0, queries, own_scores, own_values, tab, big, base = call(
        own_kernel,
        (
            jax.ShapeDtypeStruct((count, width), BF),
            jax.ShapeDtypeStruct((count, width), BF),
            jax.ShapeDtypeStruct((count, width), F32),
            jax.ShapeDtypeStruct((count, width), BF),
            jax.ShapeDtypeStruct((count, 2 * width), BF),
            jax.ShapeDtypeStruct((steps, width), F32),
            jax.ShapeDtypeStruct((8, width), F32),
        ),
        (ids, mask, rows, w_patch, site_table, probe_table, row(mask_token), row(gain_time), w_qkv_time),
        smem=(0,),
        flops=4_000_000_000,
        nbytes=8_000_000,
    )

    def attend(own, cap):
        blocks = gather(own, cap)
        sources = [
            ((me // nz + dx) % nx) * nz + (me % nz + dz) % nz for _, offsets in blocks for dx, dz in offsets
        ]
        src = jnp.stack(sources).astype(jnp.int32)
        keys = steps * cap
        return call(
            functools.partial(time_kernel, [len(o) for _, o in blocks], cap, len(blocks)),
            (
                jax.ShapeDtypeStruct((count, width + 128), BF),
                jax.ShapeDtypeStruct((1, 1), jnp.int32),
            ),
            (
                src,
                mask,
                w_patch,
                tab,
                big,
                base,
                row(gain_time),
                w_qkv_time,
                queries,
                own_scores,
                own_values,
                x0,
                w_out_time,
                *[b for b, _ in blocks],
            ),
            smem=(0,),
            smem_out=(1,),
            scratch=(
                pltpu.VMEM((PAIRS, keys, 256), BF),
                pltpu.VMEM((PAIRS, keys, 256), BF),
                pltpu.VMEM((count, width), BF),
            ),
            flops=20_000_000_000,
            nbytes=10_000_000,
        )

    x1, most = attend(packed, CAP)
    x1 = lax.cond(most[0, 0] > CAP, lambda: attend(pack(count), count)[0], lambda: x1)
    window = lax.all_to_all(x1, ("probe", "lane"), split_axis=0, concat_axis=0, tiled=True)
    done = call(
        cross_kernel,
        jax.ShapeDtypeStruct((count, width), BF),
        (window, row(gain_cross), w_qkv_cross, w_out_cross),
        scratch=(pltpu.VMEM((count, width), BF),),
        flops=2_000_000_000,
        nbytes=6_000_000,
    )
    out = lax.all_to_all(done, ("probe", "lane"), split_axis=0, concat_axis=0, tiled=True)
    return out[None, None]


def solution(mesh):
    return jax.shard_map(
        body,
        mesh=mesh,
        in_specs=(
            P("probe", "lane", "tm", None),
            P("probe", "lane", "tm"),
            P("probe", "lane"),
            P("probe"),
            P(),
            P(),
            P(),
            P(),
            P(),
            P(),
            P(),
            P(),
            P(),
            P(),
        ),
        out_specs=P("probe", "lane", "tm", None),
        check_vma=False,
    )
```

```python
import functools
import math

import jax
import jax.numpy as jnp
from jax import lax
from jax.experimental import pallas as pl
from jax.experimental.pallas import tpu as pltpu
from jax.sharding import PartitionSpec as P

HEADS = 12
HEAD_DIM = 64
WIN = 16
PAIRS = HEADS // 2
PACKED = 512
COL_TIME, COL_VALID, COL_COUNT = 480, 481, 482
CAP = 96
NX, NZ = 2, 8
FAR = -1e30
BF = jnp.bfloat16
F32 = jnp.float32
NT = (((1,), (1,)), ((), ()))


def iota(shape, dim):
    return lax.broadcasted_iota(jnp.int32, shape, dim)


def mm(a, b):
    return jnp.dot(a, b, preferred_element_type=F32)


def norm(rows, gain):
    middle = jnp.mean(rows, axis=-1, keepdims=True)
    centred = rows - middle
    spread = jnp.mean(centred * centred, axis=-1, keepdims=True)
    return centred * lax.rsqrt(spread + 1e-05) * gain


def vector(ref):
    return ref[...].astype(F32).reshape(1, -1)


def split(value):
    high = value.astype(BF)
    return high, (value - high.astype(F32)).astype(BF)


def to_column(row):
    n = row.shape[1]
    eye = iota((n, n), 0) == iota((n, n), 1)
    return jnp.sum(jnp.where(eye, row, 0.0), axis=1, keepdims=True)


def call(kernel, out, args, *, smem=(), smem_out=(), scratch=(), vmem=16, flops=0, nbytes=0):
    several = isinstance(out, tuple)
    outs = out if several else (out,)
    space = lambda i, scalars: pl.BlockSpec(memory_space=pltpu.SMEM if i in scalars else pltpu.VMEM)
    specs = tuple(space(i, smem_out) for i in range(len(outs)))
    return pl.pallas_call(
        kernel,
        out_shape=out,
        in_specs=[space(i, smem) for i in range(len(args))],
        out_specs=specs if several else specs[0],
        scratch_shapes=list(scratch),
        compiler_params=pltpu.CompilerParams(vmem_limit_bytes=vmem * 1024 * 1024),
        cost_estimate=pl.CostEstimate(flops=flops, bytes_accessed=nbytes, transcendentals=0),
    )(*args)


def pack_kernel(keep_ref, volt_ref, out_ref, wide):
    count, samples = volt_ref.shape
    cap = out_ref.shape[0]
    lane = iota((count, PACKED), 1)
    extra = jnp.where(
        lane == COL_TIME, iota((count, PACKED), 0).astype(F32), jnp.where(lane == COL_VALID, 1.0, 0.0)
    )
    wide[...] = extra.astype(BF)
    wide[:, :samples] = volt_ref[...]
    mask = keep_ref[...].astype(F32)
    upper = jnp.where(iota((count, count), 0) <= iota((count, count), 1), 1.0, 0.0).astype(BF)
    rank = mm(jnp.broadcast_to(mask, (16, count)).astype(BF), upper)[0:1, :]
    pick = (rank - 1.0 == iota((cap, count), 0).astype(F32)) & (mask > 0.5)
    packed = mm(jnp.where(pick, 1.0, 0.0).astype(BF), wide[...])
    total = jnp.sum(mask, axis=1, keepdims=True)
    out_ref[...] = jnp.where(iota(packed.shape, 1) == COL_COUNT, total, packed).astype(BF)


def frequencies(rows, half):
    return jnp.exp(iota((rows, half), 1).astype(F32) * (-math.log(10000.0) / half))


def own_kernel(
    site_id_ref,
    probe_id_ref,
    keep_ref,
    volt_ref,
    w_patch_ref,
    site_ref,
    probe_ref,
    token_ref,
    gain_ref,
    w_qkv_ref,
    x0_ref,
    q_ref,
    self_ref,
    v_ref,
    tab_ref,
    big_ref,
    base_ref,
):
    count, width = x0_ref.shape
    half = width // 2
    steps = big_ref.shape[0]
    fine = iota((count, half), 0).astype(F32) * frequencies(count, half)
    sin_l, cos_l = jnp.sin(fine), jnp.cos(fine)
    coarse = (iota((steps, half), 0) * count).astype(F32) * frequencies(steps, half)
    big_ref[:, :half] = jnp.sin(coarse)
    big_ref[:, half:] = jnp.cos(coarse)
    for at, value in ((0, sin_l), (half, cos_l)):
        high, low = split(value)
        tab_ref[:, at : at + half] = high
        tab_ref[:, width + at : width + at + half] = low
    me = lax.axis_index("tm")
    row = big_ref[pl.ds(me, 1), :]
    sin_d, cos_d = row[:, :half], row[:, half:]
    code = jnp.concatenate([sin_d * cos_l + cos_d * sin_l, cos_d * cos_l - sin_d * sin_l], axis=1)

    sites, probes = site_ref.shape[0], probe_ref.shape[0]
    one_site = jnp.where(iota((16, sites), 1) == site_id_ref[0, 0], 1.0, 0.0).astype(BF)
    one_probe = jnp.where(iota((16, probes), 1) == probe_id_ref[0], 1.0, 0.0).astype(BF)
    base = mm(one_site, site_ref[...])[0:8] + mm(one_probe, probe_ref[...])[0:8]
    base_ref[...] = base

    keep = to_column(keep_ref[...].astype(F32))
    proj = mm(volt_ref[...], w_patch_ref[...])
    proj = jnp.where(keep > 0.5, proj, vector(token_ref))
    x0 = (proj + base[0:1] + code).astype(BF)
    x0_ref[...] = x0
    h1 = norm(x0.astype(F32), vector(gain_ref)).astype(BF)
    qkv = mm(h1, w_qkv_ref[...]).astype(BF)
    queries = (qkv[:, :width].astype(F32) * (1.0 / math.sqrt(HEAD_DIM))).astype(BF)
    q_ref[...] = queries
    v_ref[...] = qkv[:, 2 * width :]
    product = queries.astype(F32) * qkv[:, width : 2 * width].astype(F32)
    same_head = jnp.where(iota((128, 128), 0) // HEAD_DIM == iota((128, 128), 1) // HEAD_DIM, 1.0, 0.0).astype(BF)
    for pair in range(PAIRS):
        cols = slice(pair * 128, pair * 128 + 128)
        high, low = split(product[:, cols])
        score = mm(high, same_head) + mm(low, same_head)
        self_ref[:, cols] = jnp.where(keep > 0.5, FAR, score)


def keys_values(rows, offsets, cap, w_patch_ref, tab_ref, big_ref, base_ref, gain, w_qkv_ref):
    total = rows.shape[0]
    count, width = tab_ref.shape[0], base_ref.shape[1]
    half = width // 2
    samples = w_patch_ref.shape[0]
    local = rows[:, 384:512].astype(F32)[:, COL_TIME - 384 : COL_TIME - 383]
    proj = mm(rows[:, :samples], w_patch_ref[...])
    pick = jnp.where(iota((total, count), 1).astype(F32) == local, 1.0, 0.0).astype(BF)
    found = mm(pick, tab_ref[...])
    found = found[:, :width] + found[:, width:]
    me = lax.axis_index("tm")
    x, z = me // NZ, lax.rem(me, NZ)
    code = []
    for i, (dx, dz) in enumerate(offsets):
        part = found[i * cap : (i + 1) * cap]
        sin_l, cos_l = part[:, :half], part[:, half:]
        source = lax.rem(x + dx, NX) * NZ + lax.rem(z + dz + NZ, NZ)
        row = big_ref[pl.ds(source, 1), :]
        sin_d, cos_d = row[:, :half], row[:, half:]
        code.append(jnp.concatenate([sin_d * cos_l + cos_d * sin_l, cos_d * cos_l - sin_d * sin_l], axis=1))
    x0 = (proj + base_ref[0:1, :] + jnp.concatenate(code, axis=0)).astype(BF)
    h1 = norm(x0.astype(F32), gain).astype(BF)
    return mm(h1, w_qkv_ref[:, width:]).astype(BF)


def counts_of(rows, cap):
    heads = [rows[at : at + 1, COL_COUNT : COL_COUNT + 1] for at in range(0, rows.shape[0], cap)]
    return [head.astype(F32) for head in heads]


def cut(offsets, cap):
    each = max(1, 512 // cap)
    return [(at, offsets[at : at + each]) for at in range(0, len(offsets), each)]


def group_kernel(offsets, cap, nblocks, w_patch_ref, tab_ref, big_ref, base_ref, gain_ref, w_qkv_ref, *rest):
    blocks = rest[:nblocks]
    kv_ref, counts_ref = rest[nblocks:]
    rows = jnp.concatenate([block[...] for block in blocks], axis=0) if nblocks > 1 else blocks[0][...]
    for at, part in cut(offsets, cap):
        span = slice(at * cap, (at + len(part)) * cap)
        kv_ref[span, :] = keys_values(
            rows[span], part, cap, w_patch_ref, tab_ref, big_ref, base_ref, vector(gain_ref), w_qkv_ref
        )
    for i, number in enumerate(counts_of(rows, cap)):
        counts_ref[i : i + 1, :] = jnp.broadcast_to(number, (1, 128))


def attend_kernel(
    offsets,
    cap,
    ngroups,
    nblocks,
    keep_ref,
    w_patch_ref,
    tab_ref,
    big_ref,
    base_ref,
    gain_ref,
    w_qkv_ref,
    q_ref,
    self_ref,
    v_ref,
    x0_ref,
    w_out_ref,
    *rest,
):
    groups, rest = rest[: 2 * ngroups], rest[2 * ngroups :]
    blocks = rest[:nblocks]
    out_ref, over_ref, kv, ctx = rest[nblocks:]
    count, width = x0_ref.shape
    rows = jnp.concatenate([block[...] for block in blocks], axis=0)
    counts, start = [], 0
    for kv_ref, counts_ref in zip(groups[::2], groups[1::2]):
        kv[start : start + kv_ref.shape[0], :] = kv_ref[...]
        start += kv_ref.shape[0]
        counts += [counts_ref[i : i + 1, 0:1] for i in range(counts_ref.shape[0])]
    for at, part in cut(offsets, cap):
        kv[start + at * cap : start + (at + len(part)) * cap, :] = keys_values(
            rows[at * cap : (at + len(part)) * cap],
            part,
            cap,
            w_patch_ref,
            tab_ref,
            big_ref,
            base_ref,
            vector(gain_ref),
            w_qkv_ref,
        )
    counts += counts_of(rows, cap)
    keys = kv.shape[0]
    place = iota((1, keys), 1)
    bias = jnp.full((1, keys), FAR, F32)
    most = counts[0]
    for i, number in enumerate(counts):
        inside = (place >= i * cap) & ((place - i * cap).astype(F32) < jnp.minimum(number, cap))
        bias = jnp.where(inside, 0.0, bias)
        most = jnp.maximum(most, number)
    over_ref[0, 0] = jnp.max(most).astype(jnp.int32)

    low = iota((count, 128), 1) < HEAD_DIM
    ones = jnp.ones((keys, 128), BF)

    def one_pair(pair):
        at = pair * 128 if isinstance(pair, int) else pl.multiple_of(pair * 128, 128)
        cols, value_cols = pl.ds(at, 128), pl.ds(width + at, 128)
        queries = q_ref[:, cols]
        zero = jnp.zeros_like(queries)
        both = jnp.concatenate([jnp.where(low, queries, zero), jnp.where(low, zero, queries)], axis=0)
        scores = lax.dot_general(both, kv[:, cols], NT, preferred_element_type=F32) + bias
        own = self_ref[:, cols]
        own = jnp.concatenate([own[:, 0:1], own[:, HEAD_DIM : HEAD_DIM + 1]], axis=0)
        top = jnp.maximum(jnp.max(scores, axis=1, keepdims=True), own)
        weights = jnp.exp(scores - top).astype(BF)
        mixed = mm(weights, jnp.concatenate([kv[:, value_cols], ones], axis=1))
        own = jnp.exp(own - top)
        total = mixed[:, 128:] + own
        own = own.astype(BF).astype(F32)
        values = v_ref[:, cols].astype(F32)
        first = (mixed[:count, :128] + own[:count] * values) / total[:count]
        second = (mixed[count:, :128] + own[count:] * values) / total[count:]
        ctx[:, cols] = jnp.where(low, first, second).astype(BF)

    if keys <= 2048:
        for pair in range(PAIRS):
            one_pair(pair)
    else:
        pl.loop(0, PAIRS)(one_pair)
    x1 = x0_ref[...].astype(F32) + mm(ctx[...], w_out_ref[...])
    out_ref[:, :width] = x1.astype(BF)
    keep = to_column(keep_ref[...].astype(F32))
    out_ref[:, width:] = jnp.broadcast_to(keep, (count, 128)).astype(BF)


def cross_kernel(x_ref, gain_ref, w_qkv_ref, w_out_ref, out_ref, ctx):
    count, width = out_ref.shape
    x1 = x_ref[:, :width].astype(F32)
    h2 = norm(x1, vector(gain_ref)).astype(BF)
    qkv = mm(h2, w_qkv_ref[...]).astype(BF)
    seen = x_ref[:, width:].astype(F32)[:, 0:1]
    eye = iota((count, count), 0) == iota((count, count), 1)
    seen = jnp.sum(jnp.where(eye, seen, 0.0), axis=0, keepdims=True)
    bias = jnp.where(eye | (seen > 0.5), 0.0, FAR)
    bias = jnp.concatenate([bias, bias], axis=0)
    lane = iota((count, 128), 1)
    low = lane < HEAD_DIM
    scale = 1.0 / math.sqrt(HEAD_DIM)
    ones = jnp.ones((count, 128), BF)
    for pair in range(PAIRS):
        at = pair * 128
        queries = (qkv[:, at : at + 128].astype(F32) * scale).astype(BF)
        zero = jnp.zeros_like(queries)
        both = jnp.concatenate([jnp.where(low, queries, zero), jnp.where(low, zero, queries)], axis=0)
        scores = lax.dot_general(both, qkv[:, width + at : width + at + 128], NT, preferred_element_type=F32)
        scores = scores + bias
        top = jnp.max(scores, axis=1, keepdims=True)
        weights = jnp.exp(scores - top).astype(BF)
        values = jnp.concatenate([qkv[:, 2 * width + at : 2 * width + at + 128], ones], axis=1)
        mixed = mm(weights, values)
        done = mixed[:, :128] / mixed[:, 128:]
        ctx[:, at : at + 128] = jnp.where(low, done[:count], done[count:]).astype(BF)
    out_ref[...] = (x1 + mm(ctx[...], w_out_ref[...])).astype(BF)


def body(
    volt,
    keep,
    site_ids,
    probe_ids,
    w_patch,
    site_table,
    probe_table,
    mask_token,
    gain_time,
    w_qkv_time,
    w_out_time,
    gain_cross,
    w_qkv_cross,
    w_out_cross,
):
    width = w_patch.shape[1]
    rows = volt[0, 0]
    count = rows.shape[0]
    mask = keep[0]
    steps = NX * NZ

    def shift(array, dx, dz):
        pairs = []
        for i in range(steps):
            x, z = divmod(i, NZ)
            pairs.append((i, ((x + dx) % NX) * NZ + (z + dz) % NZ))
        return lax.ppermute(array, "tm", pairs)

    def pack(cap):
        return call(
            pack_kernel,
            jax.ShapeDtypeStruct((cap, PACKED), BF),
            (mask, rows),
            scratch=(pltpu.VMEM((count, PACKED), BF),),
            vmem=4,
            flops=2 * cap * count * PACKED,
            nbytes=500_000,
        )

    packed = pack(CAP)
    x0, queries, own_scores, own_values, tab, big, base = call(
        own_kernel,
        (
            jax.ShapeDtypeStruct((count, width), BF),
            jax.ShapeDtypeStruct((count, width), BF),
            jax.ShapeDtypeStruct((count, width), F32),
            jax.ShapeDtypeStruct((count, width), BF),
            jax.ShapeDtypeStruct((count, 2 * width), BF),
            jax.ShapeDtypeStruct((steps, width), F32),
            jax.ShapeDtypeStruct((8, width), F32),
        ),
        (site_ids, probe_ids, mask, rows, w_patch, site_table, probe_table, mask_token, gain_time, w_qkv_time),
        smem=(0, 1),
        vmem=24,
        flops=5_000_000_000,
        nbytes=8_000_000,
    )
    shared = (w_patch, tab, big, base, gain_time, w_qkv_time)

    def attend(own, cap, vmem):
        def group(blocks, offsets):
            return call(
                functools.partial(group_kernel, offsets, cap, len(blocks)),
                (
                    jax.ShapeDtypeStruct((len(offsets) * cap, 2 * width), BF),
                    jax.ShapeDtypeStruct((len(offsets), 128), F32),
                ),
                (*shared, *blocks),
                vmem=vmem,
                flops=2_500_000_000,
                nbytes=6_000_000,
            )

        below, above, beside = shift(own, 0, 1), shift(own, 0, -1), shift(own, 1, 0)
        first = group((own, below, above, beside), [(0, 0), (0, -1), (0, 1), (1, 0)])
        down2 = shift(jnp.concatenate([below, beside], axis=0), 0, 1)
        up2 = shift(jnp.concatenate([above, beside], axis=0), 0, -1)
        second = group((down2, up2), [(0, -2), (1, -1), (0, 2), (1, 1)])
        down3, up3 = shift(down2, 0, 1), shift(up2, 0, -1)
        third = group((down3, up3), [(0, -3), (1, -2), (0, 3), (1, 2)])
        down4 = shift(down3, 0, 1)
        up4 = shift(up3[cap:], 0, -1)
        far = shift(up3[:cap], 1, -1)
        last = [(0, -4), (1, -3), (1, 3), (1, 4)]
        return call(
            functools.partial(attend_kernel, last, cap, 3, 3),
            (
                jax.ShapeDtypeStruct((count, width + 128), BF),
                jax.ShapeDtypeStruct((1, 1), jnp.int32),
            ),
            (
                mask,
                *shared,
                queries,
                own_scores,
                own_values,
                x0,
                w_out_time,
                *first,
                *second,
                *third,
                down4,
                up4,
                far,
            ),
            smem_out=(1,),
            scratch=(pltpu.VMEM((steps * cap, 2 * width), BF), pltpu.VMEM((count, width), BF)),
            vmem=vmem + 8,
            flops=12_000_000_000,
            nbytes=10_000_000,
        )

    x1, most = attend(packed, CAP, 20)
    x1 = lax.cond(most[0, 0] > CAP, lambda: attend(pack(count), count, 50)[0], lambda: x1)
    window = lax.all_to_all(x1, ("probe", "lane"), split_axis=0, concat_axis=0, tiled=True)
    done = call(
        cross_kernel,
        jax.ShapeDtypeStruct((count, width), BF),
        (window, gain_cross, w_qkv_cross, w_out_cross),
        scratch=(pltpu.VMEM((count, width), BF),),
        flops=2_000_000_000,
        nbytes=6_000_000,
    )
    out = lax.all_to_all(done, ("probe", "lane"), split_axis=0, concat_axis=0, tiled=True)
    return out[None, None]


def solution(mesh):
    return jax.shard_map(
        body,
        mesh=mesh,
        in_specs=(
            P("probe", "lane", "tm", None),
            P("probe", "lane", "tm"),
            P("probe", "lane"),
            P("probe"),
            P(),
            P(),
            P(),
            P(),
            P(),
            P(),
            P(),
            P(),
            P(),
            P(),
        ),
        out_specs=P("probe", "lane", "tm", None),
        check_vma=False,
    )
```

```python
import functools
import math

import jax
import jax.numpy as jnp
from jax import lax
from jax.experimental import pallas as pl
from jax.experimental.pallas import tpu as pltpu
from jax.sharding import PartitionSpec as P

HEADS = 12
HEAD_DIM = 64
WIN = 16
PAIRS = HEADS // 2
PACKED = 512
COL_TIME, COL_VALID, COL_COUNT = 480, 481, 482
CAP = 96
NX, NZ = 2, 8
FAR = -1e30
BF = jnp.bfloat16
F32 = jnp.float32
NT = (((1,), (1,)), ((), ()))


def iota(shape, dim):
    return lax.broadcasted_iota(jnp.int32, shape, dim)


def mm(a, b):
    return jnp.dot(a, b, preferred_element_type=F32)


def norm(rows, gain):
    middle = jnp.mean(rows, axis=-1, keepdims=True)
    centred = rows - middle
    spread = jnp.mean(centred * centred, axis=-1, keepdims=True)
    return centred * lax.rsqrt(spread + 1e-05) * gain


def vector(ref):
    return ref[...].astype(F32).reshape(1, -1)


def split(value):
    high = value.astype(BF)
    return high, (value - high.astype(F32)).astype(BF)


def to_column(row):
    n = row.shape[1]
    eye = iota((n, n), 0) == iota((n, n), 1)
    return jnp.sum(jnp.where(eye, row, 0.0), axis=1, keepdims=True)


def call(kernel, out, args, *, smem=(), smem_out=(), scratch=(), vmem=16, flops=0, nbytes=0):
    several = isinstance(out, tuple)
    outs = out if several else (out,)


    def space(i, scalars):
        where = pltpu.SMEM if i in scalars else pltpu.VMEM
        return pl.BlockSpec(memory_space=where)

    specs = tuple(space(i, smem_out) for i in range(len(outs)))
    return pl.pallas_call(
        kernel,
        out_shape=out,
        in_specs=[space(i, smem) for i in range(len(args))],
        out_specs=specs if several else specs[0],
        scratch_shapes=list(scratch),
        compiler_params=pltpu.CompilerParams(vmem_limit_bytes=vmem * 1024 * 1024),
        cost_estimate=pl.CostEstimate(flops=flops, bytes_accessed=nbytes, transcendentals=0),
    )(*args)


def pack_kernel(keep_ref, volt_ref, out_ref, wide):
    count, samples = volt_ref.shape
    cap = out_ref.shape[0]
    lane = iota((count, PACKED), 1)
    extra = jnp.where(
        lane == COL_TIME, iota((count, PACKED), 0).astype(F32), jnp.where(lane == COL_VALID, 1.0, 0.0)
    )
    wide[...] = extra.astype(BF)
    mask = keep_ref[...].astype(F32)
    upper = jnp.where(iota((count, count), 0) <= iota((count, count), 1), 1.0, 0.0).astype(BF)
    rank = mm(jnp.broadcast_to(mask, (16, count)).astype(BF), upper)[0:1, :]
    pick = (rank - 1.0 == iota((cap, count), 0).astype(F32)) & (mask > 0.5)
    total = jnp.sum(mask, axis=1, keepdims=True)
    wide[:, :samples] = volt_ref[...]
    packed = mm(jnp.where(pick, 1.0, 0.0).astype(BF), wide[...])
    out_ref[...] = jnp.where(iota(packed.shape, 1) == COL_COUNT, total, packed).astype(BF)


def frequencies(rows, half):
    return jnp.exp(iota((rows, half), 1).astype(F32) * (-math.log(10000.0) / half))


def turn(at, by):
    return at[0] * by[1] + at[1] * by[0], at[1] * by[1] - at[0] * by[0]


def waves(rows, step, half):
    angle = (iota((rows, half), 0) * step).astype(F32) * frequencies(rows, half)
    return jnp.sin(angle), jnp.cos(angle)


def table_kernel(site_id_ref, probe_id_ref, site_ref, probe_ref, tab_ref, big_ref, base_ref):
    count, width = tab_ref.shape[0], base_ref.shape[1]
    half = width // 2
    steps = big_ref.shape[0]
    big_ref[:, :half], big_ref[:, half:] = waves(steps, count, half)
    fine, middle = waves(16, 1, half), waves(count // 16, 16, half)
    for a in range(count // 16):
        at = slice(a * 16, (a + 1) * 16)
        row = [part[a : a + 1] for part in middle]
        for start, value in zip((0, half), turn(row, fine)):
            high, low = split(value)
            tab_ref[at, start : start + half] = high
            tab_ref[at, width + start : width + start + half] = low
    sites, probes = site_ref.shape[0], probe_ref.shape[0]
    one_site = jnp.where(iota((16, sites), 1) == site_id_ref[0, 0], 1.0, 0.0).astype(BF)
    one_probe = jnp.where(iota((16, probes), 1) == probe_id_ref[0], 1.0, 0.0).astype(BF)
    base_ref[...] = mm(one_site, site_ref[...])[0:8] + mm(one_probe, probe_ref[...])[0:8]


def code_of(found, source, big_ref):
    width = big_ref.shape[1]
    half = width // 2
    local = found[:, :width] + found[:, width:]
    row = big_ref[pl.ds(source, 1), :]
    return jnp.concatenate(
        turn((row[:, :half], row[:, half:]), (local[:, :half], local[:, half:])), axis=1
    )


def own_kernel(
    keep_ref,
    volt_ref,
    token_ref,
    w_patch_ref,
    tab_ref,
    big_ref,
    base_ref,
    gain_ref,
    w_qkv_ref,
    after_ref,
    x0_ref,
    q_ref,
    self_ref,
    v_ref,
):
    del after_ref
    width = x0_ref.shape[1]
    code = code_of(tab_ref[...].astype(F32), lax.axis_index("tm"), big_ref)
    keep = to_column(keep_ref[...].astype(F32))
    proj = mm(volt_ref[...], w_patch_ref[...])
    proj = jnp.where(keep > 0.5, proj, vector(token_ref))
    x0 = (proj + base_ref[0:1, :] + code).astype(BF)
    x0_ref[...] = x0
    h1 = norm(x0.astype(F32), vector(gain_ref)).astype(BF)
    qkv = mm(h1, w_qkv_ref[...]).astype(BF)
    queries = (qkv[:, :width].astype(F32) * (1.0 / math.sqrt(HEAD_DIM))).astype(BF)
    q_ref[...] = queries
    v_ref[...] = qkv[:, 2 * width :]
    product = queries.astype(F32) * qkv[:, width : 2 * width].astype(F32)
    same_head = jnp.where(iota((128, 128), 0) // HEAD_DIM == iota((128, 128), 1) // HEAD_DIM, 1.0, 0.0).astype(BF)
    for pair in range(PAIRS):
        cols = slice(pair * 128, pair * 128 + 128)
        high, low = split(product[:, cols])
        score = mm(high, same_head) + mm(low, same_head)
        self_ref[:, cols] = jnp.where(keep > 0.5, FAR, score)


def keys_values(rows, offsets, cap, w_patch_ref, tab_ref, big_ref, base_ref, gain, w_qkv_ref):
    total = rows.shape[0]
    count, width = tab_ref.shape[0], base_ref.shape[1]
    samples = w_patch_ref.shape[0]
    local = rows[:, 384:512].astype(F32)[:, COL_TIME - 384 : COL_TIME - 383]
    proj = mm(rows[:, :samples], w_patch_ref[...])
    pick = jnp.where(iota((total, count), 1).astype(F32) == local, 1.0, 0.0).astype(BF)
    found = mm(pick, tab_ref[...])
    me = lax.axis_index("tm")
    x, z = me // NZ, lax.rem(me, NZ)
    code = []
    for i, (dx, dz) in enumerate(offsets):
        source = lax.rem(x + dx, NX) * NZ + lax.rem(z + dz + NZ, NZ)
        code.append(code_of(found[i * cap : (i + 1) * cap], source, big_ref))
    x0 = (proj + base_ref[0:1, :] + jnp.concatenate(code, axis=0)).astype(BF)
    h1 = norm(x0.astype(F32), gain).astype(BF)
    return mm(h1, w_qkv_ref[:, width:]).astype(BF)


def counts_of(rows, cap):
    heads = [rows[at : at + 1, COL_COUNT : COL_COUNT + 1] for at in range(0, rows.shape[0], cap)]
    return [head.astype(F32) for head in heads]


def cut(offsets, cap):
    each = max(1, 512 // cap)
    return [(at, offsets[at : at + each]) for at in range(0, len(offsets), each)]


def group_kernel(offsets, cap, nblocks, w_patch_ref, tab_ref, big_ref, base_ref, gain_ref, w_qkv_ref, *rest):
    blocks = rest[:nblocks]
    kv_ref, counts_ref = rest[nblocks:]
    rows = jnp.concatenate([block[...] for block in blocks], axis=0) if nblocks > 1 else blocks[0][...]
    for at, part in cut(offsets, cap):
        span = slice(at * cap, (at + len(part)) * cap)
        kv_ref[span, :] = keys_values(
            rows[span], part, cap, w_patch_ref, tab_ref, big_ref, base_ref, vector(gain_ref), w_qkv_ref
        )
    for i, number in enumerate(counts_of(rows, cap)):
        counts_ref[i : i + 1, :] = jnp.broadcast_to(number, (1, 128))


def attend_kernel(
    offsets,
    cap,
    ngroups,
    nblocks,
    keep_ref,
    w_patch_ref,
    tab_ref,
    big_ref,
    base_ref,
    gain_ref,
    w_qkv_ref,
    q_ref,
    self_ref,
    v_ref,
    x0_ref,
    w_out_ref,
    later_ref,
    *rest,
):
    del later_ref
    groups, rest = rest[: 2 * ngroups], rest[2 * ngroups :]
    blocks = rest[:nblocks]
    out_ref, over_ref, kv, ctx = rest[nblocks:]
    count, width = x0_ref.shape
    rows = jnp.concatenate([block[...] for block in blocks], axis=0)
    counts, start = [], 0
    for kv_ref, counts_ref in zip(groups[::2], groups[1::2]):
        kv[start : start + kv_ref.shape[0], :] = kv_ref[...]
        start += kv_ref.shape[0]
        counts += [counts_ref[i : i + 1, 0:1] for i in range(counts_ref.shape[0])]
    for at, part in cut(offsets, cap):
        kv[start + at * cap : start + (at + len(part)) * cap, :] = keys_values(
            rows[at * cap : (at + len(part)) * cap],
            part,
            cap,
            w_patch_ref,
            tab_ref,
            big_ref,
            base_ref,
            vector(gain_ref),
            w_qkv_ref,
        )
    counts += counts_of(rows, cap)
    keys = kv.shape[0]
    place = iota((1, keys), 1)
    bias = jnp.full((1, keys), FAR, F32)
    most = counts[0]
    for i, number in enumerate(counts):
        inside = (place >= i * cap) & ((place - i * cap).astype(F32) < jnp.minimum(number, cap))
        bias = jnp.where(inside, 0.0, bias)
        most = jnp.maximum(most, number)
    over_ref[0, 0] = jnp.max(most).astype(jnp.int32)

    low = iota((count, 128), 1) < HEAD_DIM
    ones = jnp.ones((keys, 128), BF)

    def one_pair(pair):
        at = pair * 128 if isinstance(pair, int) else pl.multiple_of(pair * 128, 128)
        cols, value_cols = pl.ds(at, 128), pl.ds(width + at, 128)
        queries = q_ref[:, cols]
        zero = jnp.zeros_like(queries)
        both = jnp.concatenate([jnp.where(low, queries, zero), jnp.where(low, zero, queries)], axis=0)
        scores = lax.dot_general(both, kv[:, cols], NT, preferred_element_type=F32) + bias
        own = self_ref[:, cols]
        own = jnp.concatenate([own[:, 0:1], own[:, HEAD_DIM : HEAD_DIM + 1]], axis=0)
        top = jnp.maximum(jnp.max(scores, axis=1, keepdims=True), own)
        weights = jnp.exp(scores - top).astype(BF)
        mixed = mm(weights, jnp.concatenate([kv[:, value_cols], ones], axis=1))
        own = jnp.exp(own - top)
        total = mixed[:, 128:] + own
        own = own.astype(BF).astype(F32)
        values = v_ref[:, cols].astype(F32)
        first = (mixed[:count, :128] + own[:count] * values) / total[:count]
        second = (mixed[count:, :128] + own[count:] * values) / total[count:]
        ctx[:, cols] = jnp.where(low, first, second).astype(BF)

    if keys <= 2048:
        for pair in range(PAIRS):
            one_pair(pair)
    else:
        pl.loop(0, PAIRS)(one_pair)
    x1 = x0_ref[...].astype(F32) + mm(ctx[...], w_out_ref[...])
    out_ref[:, :width] = x1.astype(BF)
    keep = to_column(keep_ref[...].astype(F32))
    out_ref[:, width:] = jnp.broadcast_to(keep, (count, 128)).astype(BF)


def cross_kernel(x_ref, gain_ref, w_qkv_ref, w_out_ref, out_ref, ctx):
    count, width = out_ref.shape
    x1 = x_ref[:, :width].astype(F32)
    h2 = norm(x1, vector(gain_ref)).astype(BF)
    qkv = mm(h2, w_qkv_ref[...]).astype(BF)
    seen = x_ref[:, width:].astype(F32)[:, 0:1]
    eye = iota((count, count), 0) == iota((count, count), 1)
    seen = jnp.sum(jnp.where(eye, seen, 0.0), axis=0, keepdims=True)
    bias = jnp.where(eye | (seen > 0.5), 0.0, FAR)
    bias = jnp.concatenate([bias, bias], axis=0)
    lane = iota((count, 128), 1)
    low = lane < HEAD_DIM
    scale = 1.0 / math.sqrt(HEAD_DIM)
    ones = jnp.ones((count, 128), BF)
    for pair in range(PAIRS):
        at = pair * 128
        queries = (qkv[:, at : at + 128].astype(F32) * scale).astype(BF)
        zero = jnp.zeros_like(queries)
        both = jnp.concatenate([jnp.where(low, queries, zero), jnp.where(low, zero, queries)], axis=0)
        scores = lax.dot_general(both, qkv[:, width + at : width + at + 128], NT, preferred_element_type=F32)
        scores = scores + bias
        top = jnp.max(scores, axis=1, keepdims=True)
        weights = jnp.exp(scores - top).astype(BF)
        values = jnp.concatenate([qkv[:, 2 * width + at : 2 * width + at + 128], ones], axis=1)
        mixed = mm(weights, values)
        done = mixed[:, :128] / mixed[:, 128:]
        ctx[:, at : at + 128] = jnp.where(low, done[:count], done[count:]).astype(BF)
    out_ref[...] = (x1 + mm(ctx[...], w_out_ref[...])).astype(BF)


def body(
    volt,
    keep,
    site_ids,
    probe_ids,
    w_patch,
    site_table,
    probe_table,
    mask_token,
    gain_time,
    w_qkv_time,
    w_out_time,
    gain_cross,
    w_qkv_cross,
    w_out_cross,
):
    width = w_patch.shape[1]
    rows = volt[0, 0]
    count = rows.shape[0]
    mask = keep[0]
    steps = NX * NZ

    def shift(array, dx, dz):
        pairs = []
        for i in range(steps):
            x, z = divmod(i, NZ)
            pairs.append((i, ((x + dx) % NX) * NZ + (z + dz) % NZ))
        return lax.ppermute(array, "tm", pairs)

    def pack(cap):
        return call(
            pack_kernel,
            jax.ShapeDtypeStruct((cap, PACKED), BF),
            (mask, rows),
            scratch=(pltpu.VMEM((count, PACKED), BF),),
            vmem=4,
            flops=2 * cap * count * PACKED,
            nbytes=500_000,
        )

    packed = pack(CAP)
    tab, big, base = call(
        table_kernel,
        (
            jax.ShapeDtypeStruct((count, 2 * width), BF),
            jax.ShapeDtypeStruct((steps, width), F32),
            jax.ShapeDtypeStruct((8, width), F32),
        ),
        (site_ids, probe_ids, site_table, probe_table),
        smem=(0, 1),
        vmem=8,
        flops=2_000_000_000,
        nbytes=1_000_000,
    )
    shared = (w_patch, tab, big, base, gain_time, w_qkv_time)

    def own_part(after):
        return call(
            own_kernel,
            (
                jax.ShapeDtypeStruct((count, width), BF),
                jax.ShapeDtypeStruct((count, width), BF),
                jax.ShapeDtypeStruct((count, width), F32),
                jax.ShapeDtypeStruct((count, width), BF),
            ),
            (mask, rows, mask_token, *shared, after),
            vmem=24,
            flops=300_000_000,
            nbytes=100_000,
        )

    def attend(own, cap, vmem, mine=None):
        def group(blocks, offsets):
            return call(
                functools.partial(group_kernel, offsets, cap, len(blocks)),
                (
                    jax.ShapeDtypeStruct((len(offsets) * cap, 2 * width), BF),
                    jax.ShapeDtypeStruct((len(offsets), 128), F32),
                ),
                (*shared, *blocks),
                vmem=vmem,
                flops=2_500_000_000,
                nbytes=6_000_000,
            )

        below, above, beside = shift(own, 0, 1), shift(own, 0, -1), shift(own, 1, 0)
        first = group((own, below, above, beside), [(0, 0), (0, -1), (0, 1), (1, 0)])
        down2 = shift(jnp.concatenate([below, beside], axis=0), 0, 1)
        up2 = shift(jnp.concatenate([above, beside], axis=0), 0, -1)
        second = group((down2, up2), [(0, -2), (1, -1), (0, 2), (1, 1)])
        down3, up3 = shift(down2, 0, 1), shift(up2, 0, -1)
        third = group((down3, up3), [(0, -3), (1, -2), (0, 3), (1, 2)])
        down4 = shift(down3, 0, 1)
        up4 = shift(up3[cap:], 0, -1)
        far = shift(up3[:cap], 1, -1)
        mine = mine or own_part(third[1])
        x0, queries, own_scores, own_values = mine
        last = [(0, -4), (1, -3), (1, 3), (1, 4)]
        return mine, call(
            functools.partial(attend_kernel, last, cap, 3, 3),
            (
                jax.ShapeDtypeStruct((count, width + 128), BF),
                jax.ShapeDtypeStruct((1, 1), jnp.int32),
            ),
            (
                mask,
                *shared,
                queries,
                own_scores,
                own_values,
                x0,
                w_out_time,
                w_out_cross,
                *first,
                *second,
                *third,
                down4,
                up4,
                far,
            ),
            smem_out=(1,),
            scratch=(pltpu.VMEM((steps * cap, 2 * width), BF), pltpu.VMEM((count, width), BF)),
            vmem=vmem + 8,
            flops=12_000_000_000,
            nbytes=10_000_000,
        )

    mine, (x1, most) = attend(packed, CAP, 20)
    x1 = lax.cond(most[0, 0] > CAP, lambda: attend(pack(count), count, 50, mine)[1][0], lambda: x1)
    window = lax.all_to_all(x1, ("probe", "lane"), split_axis=0, concat_axis=0, tiled=True)
    done = call(
        cross_kernel,
        jax.ShapeDtypeStruct((count, width), BF),
        (window, gain_cross, w_qkv_cross, w_out_cross),
        scratch=(pltpu.VMEM((count, width), BF),),
        flops=2_000_000_000,
        nbytes=6_000_000,
    )
    out = lax.all_to_all(done, ("probe", "lane"), split_axis=0, concat_axis=0, tiled=True)
    return out[None, None]


def solution(mesh):
    return jax.shard_map(
        body,
        mesh=mesh,
        in_specs=(
            P("probe", "lane", "tm", None),
            P("probe", "lane", "tm"),
            P("probe", "lane"),
            P("probe"),
            P(),
            P(),
            P(),
            P(),
            P(),
            P(),
            P(),
            P(),
            P(),
            P(),
        ),
        out_specs=P("probe", "lane", "tm", None),
        check_vma=False,
    )
```

```python
import functools
import math

import jax
import jax.numpy as jnp
from jax import lax
from jax.experimental import pallas as pl
from jax.experimental.pallas import tpu as pltpu
from jax.sharding import PartitionSpec as P

HEADS = 12
HEAD_DIM = 64
WIN = 16
PAIRS = HEADS // 2
PACKED = 512
COL_TIME, COL_VALID, COL_COUNT = 480, 481, 482
CAP = 96
NX, NZ = 2, 8
FAR = -1e30
BF = jnp.bfloat16
F32 = jnp.float32
NT = (((1,), (1,)), ((), ()))


def iota(shape, dim):
    return lax.broadcasted_iota(jnp.int32, shape, dim)


def mm(a, b):
    return jnp.dot(a, b, preferred_element_type=F32)


def norm(rows, gain):
    middle = jnp.mean(rows, axis=-1, keepdims=True)
    centred = rows - middle
    spread = jnp.mean(centred * centred, axis=-1, keepdims=True)
    return centred * lax.rsqrt(spread + 1e-05) * gain


def vector(ref):
    return ref[...].astype(F32).reshape(1, -1)


def split(value):
    high = value.astype(BF)
    return high, (value - high.astype(F32)).astype(BF)


def to_column(row):
    n = row.shape[1]
    eye = iota((n, n), 0) == iota((n, n), 1)
    return jnp.sum(jnp.where(eye, row, 0.0), axis=1, keepdims=True)


def call(kernel, out, args, *, smem=(), far=(), smem_out=(), scratch=(), vmem=16, flops=0, nbytes=0):
    several = isinstance(out, tuple)
    outs = out if several else (out,)


    def space(i, scalars, far=()):
        where = pltpu.SMEM if i in scalars else pl.ANY if i in far else pltpu.VMEM
        return pl.BlockSpec(memory_space=where)

    specs = tuple(space(i, smem_out) for i in range(len(outs)))
    return pl.pallas_call(
        kernel,
        out_shape=out,
        in_specs=[space(i, smem, far) for i in range(len(args))],
        out_specs=specs if several else specs[0],
        scratch_shapes=list(scratch),
        compiler_params=pltpu.CompilerParams(vmem_limit_bytes=vmem * 1024 * 1024),
        cost_estimate=pl.CostEstimate(flops=flops, bytes_accessed=nbytes, transcendentals=0),
    )(*args)


def pack_kernel(keep_ref, volt_ref, out_ref, wide):
    count, samples = volt_ref.shape
    cap = out_ref.shape[0]
    lane = iota((count, PACKED), 1)
    extra = jnp.where(
        lane == COL_TIME, iota((count, PACKED), 0).astype(F32), jnp.where(lane == COL_VALID, 1.0, 0.0)
    )
    wide[...] = extra.astype(BF)
    mask = keep_ref[...].astype(F32)
    upper = jnp.where(iota((count, count), 0) <= iota((count, count), 1), 1.0, 0.0).astype(BF)
    rank = mm(jnp.broadcast_to(mask, (16, count)).astype(BF), upper)[0:1, :]
    pick = (rank - 1.0 == iota((cap, count), 0).astype(F32)) & (mask > 0.5)
    total = jnp.sum(mask, axis=1, keepdims=True)
    wide[:, :samples] = volt_ref[...]
    packed = mm(jnp.where(pick, 1.0, 0.0).astype(BF), wide[...])
    out_ref[...] = jnp.where(iota(packed.shape, 1) == COL_COUNT, total, packed).astype(BF)


def frequencies(rows, half):
    return jnp.exp(iota((rows, half), 1).astype(F32) * (-math.log(10000.0) / half))


def turn(at, by):
    return at[0] * by[1] + at[1] * by[0], at[1] * by[1] - at[0] * by[0]


def waves(rows, step, half):
    angle = (iota((rows, half), 0) * step).astype(F32) * frequencies(rows, half)
    return jnp.sin(angle), jnp.cos(angle)


def table_kernel(site_id_ref, probe_id_ref, site_ref, probe_ref, tab_ref, big_ref, base_ref):
    count, width = tab_ref.shape[0], base_ref.shape[1]
    half = width // 2
    steps = big_ref.shape[0]
    big_ref[:, :half], big_ref[:, half:] = waves(steps, count, half)
    fine, middle = waves(16, 1, half), waves(count // 16, 16, half)
    for a in range(count // 16):
        at = slice(a * 16, (a + 1) * 16)
        row = [part[a : a + 1] for part in middle]
        for start, value in zip((0, half), turn(row, fine)):
            high, low = split(value)
            tab_ref[at, start : start + half] = high
            tab_ref[at, width + start : width + start + half] = low
    sites, probes = site_ref.shape[0], probe_ref.shape[0]
    one_site = jnp.where(iota((16, sites), 1) == site_id_ref[0, 0], 1.0, 0.0).astype(BF)
    one_probe = jnp.where(iota((16, probes), 1) == probe_id_ref[0], 1.0, 0.0).astype(BF)
    base_ref[...] = mm(one_site, site_ref[...])[0:8] + mm(one_probe, probe_ref[...])[0:8]


def code_of(found, source, big_ref):
    width = big_ref.shape[1]
    half = width // 2
    local = found[:, :width] + found[:, width:]
    row = big_ref[pl.ds(source, 1), :]
    return jnp.concatenate(
        turn((row[:, :half], row[:, half:]), (local[:, :half], local[:, half:])), axis=1
    )


def own_kernel(
    keep_ref,
    volt_ref,
    token_ref,
    w_patch_ref,
    tab_ref,
    big_ref,
    base_ref,
    gain_ref,
    w_qkv_ref,
    after_ref,
    x0_ref,
    q_ref,
    self_ref,
    v_ref,
):
    del after_ref
    width = x0_ref.shape[1]
    code = code_of(tab_ref[...].astype(F32), lax.axis_index("tm"), big_ref)
    keep = to_column(keep_ref[...].astype(F32))
    proj = mm(volt_ref[...], w_patch_ref[...])
    proj = jnp.where(keep > 0.5, proj, vector(token_ref))
    x0 = (proj + base_ref[0:1, :] + code).astype(BF)
    x0_ref[...] = x0
    h1 = norm(x0.astype(F32), vector(gain_ref)).astype(BF)
    qkv = mm(h1, w_qkv_ref[...]).astype(BF)
    queries = (qkv[:, :width].astype(F32) * (1.0 / math.sqrt(HEAD_DIM))).astype(BF)
    q_ref[...] = queries
    v_ref[...] = qkv[:, 2 * width :]
    product = queries.astype(F32) * qkv[:, width : 2 * width].astype(F32)
    same_head = jnp.where(iota((128, 128), 0) // HEAD_DIM == iota((128, 128), 1) // HEAD_DIM, 1.0, 0.0).astype(BF)
    for pair in range(PAIRS):
        cols = slice(pair * 128, pair * 128 + 128)
        high, low = split(product[:, cols])
        score = mm(high, same_head) + mm(low, same_head)
        self_ref[:, cols] = jnp.where(keep > 0.5, FAR, score)


def keys_values(rows, offsets, cap, w_patch_ref, tab_ref, big_ref, base_ref, gain, w_qkv_ref):
    total = rows.shape[0]
    count, width = tab_ref.shape[0], base_ref.shape[1]
    samples = w_patch_ref.shape[0]
    local = rows[:, 384:512].astype(F32)[:, COL_TIME - 384 : COL_TIME - 383]
    proj = mm(rows[:, :samples], w_patch_ref[...])
    pick = jnp.where(iota((total, count), 1).astype(F32) == local, 1.0, 0.0).astype(BF)
    found = mm(pick, tab_ref[...])
    me = lax.axis_index("tm")
    x, z = me // NZ, lax.rem(me, NZ)
    code = []
    for i, (dx, dz) in enumerate(offsets):
        source = lax.rem(x + dx, NX) * NZ + lax.rem(z + dz + NZ, NZ)
        code.append(code_of(found[i * cap : (i + 1) * cap], source, big_ref))
    x0 = (proj + base_ref[0:1, :] + jnp.concatenate(code, axis=0)).astype(BF)
    h1 = norm(x0.astype(F32), gain).astype(BF)
    return mm(h1, w_qkv_ref[:, width:]).astype(BF)


def counts_of(rows, cap):
    heads = [rows[at : at + 1, COL_COUNT : COL_COUNT + 1] for at in range(0, rows.shape[0], cap)]
    return [head.astype(F32) for head in heads]


def cut(offsets, cap):
    each = max(1, 512 // cap)
    return [(at, offsets[at : at + each]) for at in range(0, len(offsets), each)]


def group_kernel(offsets, cap, nblocks, w_patch_ref, tab_ref, big_ref, base_ref, gain_ref, w_qkv_ref, *rest):
    blocks = rest[:nblocks]
    kv_ref, counts_ref = rest[nblocks:]
    rows = jnp.concatenate([block[...] for block in blocks], axis=0) if nblocks > 1 else blocks[0][...]
    for at, part in cut(offsets, cap):
        span = slice(at * cap, (at + len(part)) * cap)
        kv_ref[span, :] = keys_values(
            rows[span], part, cap, w_patch_ref, tab_ref, big_ref, base_ref, vector(gain_ref), w_qkv_ref
        )
    for i, number in enumerate(counts_of(rows, cap)):
        counts_ref[i : i + 1, :] = jnp.broadcast_to(number, (1, 128))


def attend_kernel(
    offsets,
    cap,
    ngroups,
    nblocks,
    keep_ref,
    w_patch_ref,
    tab_ref,
    big_ref,
    base_ref,
    gain_ref,
    w_qkv_ref,
    q_ref,
    self_ref,
    v_ref,
    x0_ref,
    w_out_ref,
    *rest,
):
    groups, rest = rest[: 2 * ngroups], rest[2 * ngroups :]
    blocks = rest[:nblocks]
    out_ref, kv, ctx = rest[nblocks:]
    count, width = x0_ref.shape
    rows = jnp.concatenate([block[...] for block in blocks], axis=0)
    counts, start = [], 0
    for kv_ref, counts_ref in zip(groups[::2], groups[1::2]):
        kv[start : start + kv_ref.shape[0], :] = kv_ref[...]
        start += kv_ref.shape[0]
        counts += [counts_ref[i : i + 1, 0:1] for i in range(counts_ref.shape[0])]
    for at, part in cut(offsets, cap):
        kv[start + at * cap : start + (at + len(part)) * cap, :] = keys_values(
            rows[at * cap : (at + len(part)) * cap],
            part,
            cap,
            w_patch_ref,
            tab_ref,
            big_ref,
            base_ref,
            vector(gain_ref),
            w_qkv_ref,
        )
    counts += counts_of(rows, cap)
    keys = kv.shape[0]
    place = iota((1, keys), 1)
    bias = jnp.full((1, keys), FAR, F32)
    most = counts[0]
    for i, number in enumerate(counts):
        inside = (place >= i * cap) & ((place - i * cap).astype(F32) < jnp.minimum(number, cap))
        bias = jnp.where(inside, 0.0, bias)
        most = jnp.maximum(most, number)

    low = iota((count, 128), 1) < HEAD_DIM
    ones = jnp.ones((keys, 128), BF)

    def one_pair(pair):
        at = pair * 128 if isinstance(pair, int) else pl.multiple_of(pair * 128, 128)
        cols, value_cols = pl.ds(at, 128), pl.ds(width + at, 128)
        queries = q_ref[:, cols]
        zero = jnp.zeros_like(queries)
        both = jnp.concatenate([jnp.where(low, queries, zero), jnp.where(low, zero, queries)], axis=0)
        scores = lax.dot_general(both, kv[:, cols], NT, preferred_element_type=F32) + bias
        own = self_ref[:, cols]
        own = jnp.concatenate([own[:, 0:1], own[:, HEAD_DIM : HEAD_DIM + 1]], axis=0)
        top = jnp.maximum(jnp.max(scores, axis=1, keepdims=True), own)
        weights = jnp.exp(scores - top).astype(BF)
        mixed = mm(weights, jnp.concatenate([kv[:, value_cols], ones], axis=1))
        own = jnp.exp(own - top)
        total = mixed[:, 128:] + own
        own = own.astype(BF).astype(F32)
        values = v_ref[:, cols].astype(F32)
        first = (mixed[:count, :128] + own[:count] * values) / total[:count]
        second = (mixed[count:, :128] + own[count:] * values) / total[count:]
        ctx[:, cols] = jnp.where(low, first, second).astype(BF)

    if keys <= 2048:
        for pair in range(PAIRS):
            one_pair(pair)
    else:
        pl.loop(0, PAIRS)(one_pair)
    x1 = x0_ref[...].astype(F32) + mm(ctx[...], w_out_ref[...])
    out_ref[:, :width] = x1.astype(BF)
    keep = to_column(keep_ref[...].astype(F32))
    over = jnp.where(most > cap, 1.0, 0.0)
    out_ref[:, width:] = jnp.where(iota((count, 128), 1) == 0, keep, over).astype(BF)


def cross_kernel(x_ref, gain_ref, w_qkv_ref, far_w_out_ref, out_ref, over_ref, ctx, w_out_ref, sem):
    fetch = pltpu.make_async_copy(far_w_out_ref, w_out_ref, sem)
    fetch.start()
    count, width = out_ref.shape
    over_ref[0, 0] = jnp.max(x_ref[:, width:].astype(F32)[:, 1:2]).astype(jnp.int32)
    x1 = x_ref[:, :width].astype(F32)
    h2 = norm(x1, vector(gain_ref)).astype(BF)
    qkv = mm(h2, w_qkv_ref[...]).astype(BF)
    seen = x_ref[:, width:].astype(F32)[:, 0:1]
    eye = iota((count, count), 0) == iota((count, count), 1)
    seen = jnp.sum(jnp.where(eye, seen, 0.0), axis=0, keepdims=True)
    bias = jnp.where(eye | (seen > 0.5), 0.0, FAR)
    bias = jnp.concatenate([bias, bias], axis=0)
    lane = iota((count, 128), 1)
    low = lane < HEAD_DIM
    scale = 1.0 / math.sqrt(HEAD_DIM)
    ones = jnp.ones((count, 128), BF)
    for pair in range(PAIRS):
        at = pair * 128
        queries = (qkv[:, at : at + 128].astype(F32) * scale).astype(BF)
        zero = jnp.zeros_like(queries)
        both = jnp.concatenate([jnp.where(low, queries, zero), jnp.where(low, zero, queries)], axis=0)
        scores = lax.dot_general(both, qkv[:, width + at : width + at + 128], NT, preferred_element_type=F32)
        scores = scores + bias
        top = jnp.max(scores, axis=1, keepdims=True)
        weights = jnp.exp(scores - top).astype(BF)
        values = jnp.concatenate([qkv[:, 2 * width + at : 2 * width + at + 128], ones], axis=1)
        mixed = mm(weights, values)
        done = mixed[:, :128] / mixed[:, 128:]
        ctx[:, at : at + 128] = jnp.where(low, done[:count], done[count:]).astype(BF)
    fetch.wait()
    out_ref[...] = (x1 + mm(ctx[...], w_out_ref[...])).astype(BF)


def body(
    volt,
    keep,
    site_ids,
    probe_ids,
    w_patch,
    site_table,
    probe_table,
    mask_token,
    gain_time,
    w_qkv_time,
    w_out_time,
    gain_cross,
    w_qkv_cross,
    w_out_cross,
):
    width = w_patch.shape[1]
    rows = volt[0, 0]
    count = rows.shape[0]
    mask = keep[0]
    steps = NX * NZ

    def shift(array, dx, dz):
        pairs = []
        for i in range(steps):
            x, z = divmod(i, NZ)
            pairs.append((i, ((x + dx) % NX) * NZ + (z + dz) % NZ))
        return lax.ppermute(array, "tm", pairs)

    def pack(cap):
        return call(
            pack_kernel,
            jax.ShapeDtypeStruct((cap, PACKED), BF),
            (mask, rows),
            scratch=(pltpu.VMEM((count, PACKED), BF),),
            vmem=4,
            flops=2 * cap * count * PACKED,
            nbytes=500_000,
        )

    packed = pack(CAP)
    tab, big, base = call(
        table_kernel,
        (
            jax.ShapeDtypeStruct((count, 2 * width), BF),
            jax.ShapeDtypeStruct((steps, width), F32),
            jax.ShapeDtypeStruct((8, width), F32),
        ),
        (site_ids, probe_ids, site_table, probe_table),
        smem=(0, 1),
        vmem=8,
        flops=2_000_000_000,
        nbytes=1_000_000,
    )
    shared = (w_patch, tab, big, base, gain_time, w_qkv_time)

    def own_part(after):
        return call(
            own_kernel,
            (
                jax.ShapeDtypeStruct((count, width), BF),
                jax.ShapeDtypeStruct((count, width), BF),
                jax.ShapeDtypeStruct((count, width), F32),
                jax.ShapeDtypeStruct((count, width), BF),
            ),
            (mask, rows, mask_token, *shared, after),
            vmem=24,
            flops=300_000_000,
            nbytes=100_000,
        )

    def attend(own, cap, vmem, mine=None):
        def group(blocks, offsets):
            return call(
                functools.partial(group_kernel, offsets, cap, len(blocks)),
                (
                    jax.ShapeDtypeStruct((len(offsets) * cap, 2 * width), BF),
                    jax.ShapeDtypeStruct((len(offsets), 128), F32),
                ),
                (*shared, *blocks),
                vmem=vmem,
                flops=2_500_000_000,
                nbytes=6_000_000,
            )

        below, above, beside = shift(own, 0, 1), shift(own, 0, -1), shift(own, 1, 0)
        first = group((own, below, above, beside), [(0, 0), (0, -1), (0, 1), (1, 0)])
        down2 = shift(jnp.concatenate([below, beside], axis=0), 0, 1)
        up2 = shift(jnp.concatenate([above, beside], axis=0), 0, -1)
        second = group((down2, up2), [(0, -2), (1, -1), (0, 2), (1, 1)])
        down3, up3 = shift(down2, 0, 1), shift(up2, 0, -1)
        third = group((down3, up3), [(0, -3), (1, -2), (0, 3), (1, 2)])
        down4 = shift(down3, 0, 1)
        up4 = shift(up3[cap:], 0, -1)
        far = shift(up3[:cap], 1, -1)
        mine = mine or own_part(third[1])
        x0, queries, own_scores, own_values = mine
        last = [(0, -4), (1, -3), (1, 3), (1, 4)]
        return mine, call(
            functools.partial(attend_kernel, last, cap, 3, 3),
            jax.ShapeDtypeStruct((count, width + 128), BF),
            (
                mask,
                *shared,
                queries,
                own_scores,
                own_values,
                x0,
                w_out_time,
                *first,
                *second,
                *third,
                down4,
                up4,
                far,
            ),
            scratch=(pltpu.VMEM((steps * cap, 2 * width), BF), pltpu.VMEM((count, width), BF)),
            vmem=vmem + 8,
            flops=12_000_000_000,
            nbytes=10_000_000,
        )

    def trade(array):
        return lax.all_to_all(array, ("probe", "lane"), split_axis=0, concat_axis=0, tiled=True)

    def cross(window):
        return call(
            cross_kernel,
            (jax.ShapeDtypeStruct((count, width), BF), jax.ShapeDtypeStruct((1, 1), jnp.int32)),
            (window, gain_cross, w_qkv_cross, w_out_cross),
            far=(3,),
            smem_out=(1,),
            scratch=(
                pltpu.VMEM((count, width), BF),
                pltpu.VMEM(w_out_cross.shape, BF),
                pltpu.SemaphoreType.DMA,
            ),
            flops=2_000_000_000,
            nbytes=6_000_000,
        )

    mine, x1 = attend(packed, CAP, 20)
    done, over = cross(trade(x1))
    general = over[0, 0] > 0

    def trade_by_pairs(array):
        parts = count // WIN
        here = lax.axis_index("probe") * lax.axis_size("lane") + lax.axis_index("lane")
        out = array
        for k in range(1, parts):
            there = (here ^ k) * WIN
            part = lax.dynamic_slice_in_dim(array, there, WIN, 0)
            part = lax.ppermute(part, ("probe", "lane"), [(i, i ^ k) for i in range(parts)])
            out = lax.dynamic_update_slice_in_dim(out, part, there, 0)
        return out

    def again():
        return trade_by_pairs(cross(trade_by_pairs(attend(pack(count), count, 50, mine)[1]))[0])

    out = trade(done)
    out = jnp.where(general, lax.cond(general, again, lambda: done), out)
    return out[None, None]


def solution(mesh):
    return jax.shard_map(
        body,
        mesh=mesh,
        in_specs=(
            P("probe", "lane", "tm", None),
            P("probe", "lane", "tm"),
            P("probe", "lane"),
            P("probe"),
            P(),
            P(),
            P(),
            P(),
            P(),
            P(),
            P(),
            P(),
            P(),
            P(),
        ),
        out_specs=P("probe", "lane", "tm", None),
        check_vma=False,
    )
```

```python
import functools
import math

import jax
import jax.numpy as jnp
from jax import lax
from jax.experimental import pallas as pl
from jax.experimental.pallas import tpu as pltpu
from jax.sharding import PartitionSpec as P

HEADS = 12
HEAD_DIM = 64
WIN = 16
PAIRS = HEADS // 2
PACKED = 512
COL_TIME, COL_VALID, COL_COUNT = 480, 481, 482
CAP = 96
NX, NZ = 2, 8
FAR = -1e30
BF = jnp.bfloat16
F32 = jnp.float32
NT = (((1,), (1,)), ((), ()))


def iota(shape, dim):
    return lax.broadcasted_iota(jnp.int32, shape, dim)


def mm(a, b):
    return jnp.dot(a, b, preferred_element_type=F32)


def norm(rows, gain):
    middle = jnp.mean(rows, axis=-1, keepdims=True)
    centred = rows - middle
    spread = jnp.mean(centred * centred, axis=-1, keepdims=True)
    return centred * lax.rsqrt(spread + 1e-05) * gain


def vector(ref):
    return ref[...].astype(F32).reshape(1, -1)


def split(value):
    high = value.astype(BF)
    return high, (value - high.astype(F32)).astype(BF)


def to_column(row):
    n = row.shape[1]
    eye = iota((n, n), 0) == iota((n, n), 1)
    return jnp.sum(jnp.where(eye, row, 0.0), axis=1, keepdims=True)


def call(kernel, out, args, *, smem=(), smem_out=(), scratch=(), vmem=16, flops=0, nbytes=0):
    several = isinstance(out, tuple)
    outs = out if several else (out,)


    def space(i, scalars):
        where = pltpu.SMEM if i in scalars else pltpu.VMEM
        return pl.BlockSpec(memory_space=where)

    specs = tuple(space(i, smem_out) for i in range(len(outs)))
    return pl.pallas_call(
        kernel,
        out_shape=out,
        in_specs=[space(i, smem) for i in range(len(args))],
        out_specs=specs if several else specs[0],
        scratch_shapes=list(scratch),
        compiler_params=pltpu.CompilerParams(vmem_limit_bytes=vmem * 1024 * 1024),
        cost_estimate=pl.CostEstimate(flops=flops, bytes_accessed=nbytes, transcendentals=0),
    )(*args)


def pack_kernel(keep_ref, volt_ref, out_ref, wide):
    count, samples = volt_ref.shape
    cap = out_ref.shape[0]
    lane = iota((count, PACKED), 1)
    extra = jnp.where(
        lane == COL_TIME, iota((count, PACKED), 0).astype(F32), jnp.where(lane == COL_VALID, 1.0, 0.0)
    )
    wide[...] = extra.astype(BF)
    mask = keep_ref[...].astype(F32)
    upper = jnp.where(iota((count, count), 0) <= iota((count, count), 1), 1.0, 0.0).astype(BF)
    rank = mm(jnp.broadcast_to(mask, (16, count)).astype(BF), upper)[0:1, :]
    pick = (rank - 1.0 == iota((cap, count), 0).astype(F32)) & (mask > 0.5)
    total = jnp.sum(mask, axis=1, keepdims=True)
    wide[:, :samples] = volt_ref[...]
    packed = mm(jnp.where(pick, 1.0, 0.0).astype(BF), wide[...])
    out_ref[...] = jnp.where(iota(packed.shape, 1) == COL_COUNT, total, packed).astype(BF)


def frequencies(rows, half):
    return jnp.exp(iota((rows, half), 1).astype(F32) * (-math.log(10000.0) / half))


def turn(at, by):
    return at[0] * by[1] + at[1] * by[0], at[1] * by[1] - at[0] * by[0]


def waves(rows, step, half):
    angle = (iota((rows, half), 0) * step).astype(F32) * frequencies(rows, half)
    return jnp.sin(angle), jnp.cos(angle)


def table_kernel(site_id_ref, probe_id_ref, site_ref, probe_ref, tab_ref, big_ref, base_ref):
    count, width = tab_ref.shape[0], base_ref.shape[1]
    half = width // 2
    steps = big_ref.shape[0]
    big_ref[:, :half], big_ref[:, half:] = waves(steps, count, half)
    fine, middle = waves(16, 1, half), waves(count // 16, 16, half)
    for a in range(count // 16):
        at = slice(a * 16, (a + 1) * 16)
        row = [part[a : a + 1] for part in middle]
        for start, value in zip((0, half), turn(row, fine)):
            high, low = split(value)
            tab_ref[at, start : start + half] = high
            tab_ref[at, width + start : width + start + half] = low
    sites, probes = site_ref.shape[0], probe_ref.shape[0]
    one_site = jnp.where(iota((16, sites), 1) == site_id_ref[0, 0], 1.0, 0.0).astype(BF)
    one_probe = jnp.where(iota((16, probes), 1) == probe_id_ref[0], 1.0, 0.0).astype(BF)
    base_ref[...] = mm(one_site, site_ref[...])[0:8] + mm(one_probe, probe_ref[...])[0:8]


def code_of(found, source, big_ref):
    width = big_ref.shape[1]
    half = width // 2
    local = found[:, :width] + found[:, width:]
    row = big_ref[pl.ds(source, 1), :]
    return jnp.concatenate(
        turn((row[:, :half], row[:, half:]), (local[:, :half], local[:, half:])), axis=1
    )


def own_kernel(
    keep_ref,
    volt_ref,
    token_ref,
    w_patch_ref,
    tab_ref,
    big_ref,
    base_ref,
    gain_ref,
    w_qkv_ref,
    after_ref,
    x0_ref,
    q_ref,
    self_ref,
    v_ref,
):
    del after_ref
    width = x0_ref.shape[1]
    code = code_of(tab_ref[...].astype(F32), lax.axis_index("tm"), big_ref)
    keep = to_column(keep_ref[...].astype(F32))
    proj = mm(volt_ref[...], w_patch_ref[...])
    proj = jnp.where(keep > 0.5, proj, vector(token_ref))
    x0 = (proj + base_ref[0:1, :] + code).astype(BF)
    x0_ref[...] = x0
    h1 = norm(x0.astype(F32), vector(gain_ref)).astype(BF)
    qkv = mm(h1, w_qkv_ref[...]).astype(BF)
    queries = (qkv[:, :width].astype(F32) * (1.0 / math.sqrt(HEAD_DIM))).astype(BF)
    q_ref[...] = queries
    v_ref[...] = qkv[:, 2 * width :]
    product = queries.astype(F32) * qkv[:, width : 2 * width].astype(F32)
    same_head = jnp.where(iota((128, 128), 0) // HEAD_DIM == iota((128, 128), 1) // HEAD_DIM, 1.0, 0.0).astype(BF)
    for pair in range(PAIRS):
        cols = slice(pair * 128, pair * 128 + 128)
        high, low = split(product[:, cols])
        score = mm(high, same_head) + mm(low, same_head)
        self_ref[:, cols] = jnp.where(keep > 0.5, FAR, score)


def keys_values(rows, offsets, cap, w_patch_ref, tab_ref, big_ref, base_ref, gain, w_qkv_ref):
    total = rows.shape[0]
    count, width = tab_ref.shape[0], base_ref.shape[1]
    samples = w_patch_ref.shape[0]
    local = rows[:, 384:512].astype(F32)[:, COL_TIME - 384 : COL_TIME - 383]
    proj = mm(rows[:, :samples], w_patch_ref[...])
    pick = jnp.where(iota((total, count), 1).astype(F32) == local, 1.0, 0.0).astype(BF)
    found = mm(pick, tab_ref[...])
    me = lax.axis_index("tm")
    x, z = me // NZ, lax.rem(me, NZ)
    code = []
    for i, (dx, dz) in enumerate(offsets):
        source = lax.rem(x + dx, NX) * NZ + lax.rem(z + dz + NZ, NZ)
        code.append(code_of(found[i * cap : (i + 1) * cap], source, big_ref))
    x0 = (proj + base_ref[0:1, :] + jnp.concatenate(code, axis=0)).astype(BF)
    h1 = norm(x0.astype(F32), gain).astype(BF)
    return mm(h1, w_qkv_ref[:, width:]).astype(BF)


def counts_of(rows, cap):
    heads = [rows[at : at + 1, COL_COUNT : COL_COUNT + 1] for at in range(0, rows.shape[0], cap)]
    return [head.astype(F32) for head in heads]


def cut(offsets, cap):
    each = max(1, 512 // cap)
    return [(at, offsets[at : at + each]) for at in range(0, len(offsets), each)]


def group_kernel(offsets, cap, nblocks, w_patch_ref, tab_ref, big_ref, base_ref, gain_ref, w_qkv_ref, *rest):
    blocks = rest[:nblocks]
    kv_ref, counts_ref = rest[nblocks:]
    rows = jnp.concatenate([block[...] for block in blocks], axis=0) if nblocks > 1 else blocks[0][...]
    for at, part in cut(offsets, cap):
        span = slice(at * cap, (at + len(part)) * cap)
        kv_ref[span, :] = keys_values(
            rows[span], part, cap, w_patch_ref, tab_ref, big_ref, base_ref, vector(gain_ref), w_qkv_ref
        )
    for i, number in enumerate(counts_of(rows, cap)):
        counts_ref[i : i + 1, :] = jnp.broadcast_to(number, (1, 128))


def attend_kernel(
    offsets,
    cap,
    ngroups,
    nblocks,
    keep_ref,
    w_patch_ref,
    tab_ref,
    big_ref,
    base_ref,
    gain_ref,
    w_qkv_ref,
    q_ref,
    self_ref,
    v_ref,
    x0_ref,
    w_out_ref,
    *rest,
):
    groups, rest = rest[: 2 * ngroups], rest[2 * ngroups :]
    blocks = rest[:nblocks]
    out_ref, kv, ctx = rest[nblocks:]
    count, width = x0_ref.shape
    rows = jnp.concatenate([block[...] for block in blocks], axis=0)
    counts, start = [], 0
    for kv_ref, counts_ref in zip(groups[::2], groups[1::2]):
        kv[start : start + kv_ref.shape[0], :] = kv_ref[...]
        start += kv_ref.shape[0]
        counts += [counts_ref[i : i + 1, 0:1] for i in range(counts_ref.shape[0])]
    for at, part in cut(offsets, cap):
        kv[start + at * cap : start + (at + len(part)) * cap, :] = keys_values(
            rows[at * cap : (at + len(part)) * cap],
            part,
            cap,
            w_patch_ref,
            tab_ref,
            big_ref,
            base_ref,
            vector(gain_ref),
            w_qkv_ref,
        )
    counts += counts_of(rows, cap)
    keys = kv.shape[0]
    place = iota((1, keys), 1)
    bias = jnp.full((1, keys), FAR, F32)
    most = counts[0]
    for i, number in enumerate(counts):
        inside = (place >= i * cap) & ((place - i * cap).astype(F32) < jnp.minimum(number, cap))
        bias = jnp.where(inside, 0.0, bias)
        most = jnp.maximum(most, number)

    low = iota((count, 128), 1) < HEAD_DIM
    ones = jnp.ones((keys, 128), BF)

    def one_pair(pair):
        at = pair * 128 if isinstance(pair, int) else pl.multiple_of(pair * 128, 128)
        cols, value_cols = pl.ds(at, 128), pl.ds(width + at, 128)
        queries = q_ref[:, cols]
        zero = jnp.zeros_like(queries)
        both = jnp.concatenate([jnp.where(low, queries, zero), jnp.where(low, zero, queries)], axis=0)
        scores = lax.dot_general(both, kv[:, cols], NT, preferred_element_type=F32) + bias
        own = self_ref[:, cols]
        own = jnp.concatenate([own[:, 0:1], own[:, HEAD_DIM : HEAD_DIM + 1]], axis=0)
        top = jnp.maximum(jnp.max(scores, axis=1, keepdims=True), own)
        weights = jnp.exp(scores - top).astype(BF)
        mixed = mm(weights, jnp.concatenate([kv[:, value_cols], ones], axis=1))
        own = jnp.exp(own - top)
        total = mixed[:, 128:] + own
        own = own.astype(BF).astype(F32)
        values = v_ref[:, cols].astype(F32)
        first = (mixed[:count, :128] + own[:count] * values) / total[:count]
        second = (mixed[count:, :128] + own[count:] * values) / total[count:]
        ctx[:, cols] = jnp.where(low, first, second).astype(BF)

    if keys <= 2048:
        for pair in range(PAIRS):
            one_pair(pair)
    else:
        pl.loop(0, PAIRS)(one_pair)
    x1 = x0_ref[...].astype(F32) + mm(ctx[...], w_out_ref[...])
    out_ref[:, :width] = x1.astype(BF)
    keep = to_column(keep_ref[...].astype(F32))
    over = jnp.where(most > cap, 1.0, 0.0)
    out_ref[:, width:] = jnp.where(iota((count, 128), 1) == 0, keep, over).astype(BF)


def cross_kernel(x_ref, gain_ref, w_qkv_ref, w_out_ref, out_ref, over_ref, ctx):
    count, width = out_ref.shape
    over_ref[0, 0] = jnp.max(x_ref[:, width:].astype(F32)[:, 1:2]).astype(jnp.int32)
    x1 = x_ref[:, :width].astype(F32)
    h2 = norm(x1, vector(gain_ref)).astype(BF)
    qkv = mm(h2, w_qkv_ref[...]).astype(BF)
    seen = x_ref[:, width:].astype(F32)[:, 0:1]
    eye = iota((count, count), 0) == iota((count, count), 1)
    seen = jnp.sum(jnp.where(eye, seen, 0.0), axis=0, keepdims=True)
    bias = jnp.where(eye | (seen > 0.5), 0.0, FAR)
    bias = jnp.concatenate([bias, bias], axis=0)
    lane = iota((count, 128), 1)
    low = lane < HEAD_DIM
    scale = 1.0 / math.sqrt(HEAD_DIM)
    ones = jnp.ones((count, 128), BF)
    for pair in range(PAIRS):
        at = pair * 128
        queries = (qkv[:, at : at + 128].astype(F32) * scale).astype(BF)
        zero = jnp.zeros_like(queries)
        both = jnp.concatenate([jnp.where(low, queries, zero), jnp.where(low, zero, queries)], axis=0)
        scores = lax.dot_general(both, qkv[:, width + at : width + at + 128], NT, preferred_element_type=F32)
        scores = scores + bias
        top = jnp.max(scores, axis=1, keepdims=True)
        weights = jnp.exp(scores - top).astype(BF)
        values = jnp.concatenate([qkv[:, 2 * width + at : 2 * width + at + 128], ones], axis=1)
        mixed = mm(weights, values)
        done = mixed[:, :128] / mixed[:, 128:]
        ctx[:, at : at + 128] = jnp.where(low, done[:count], done[count:]).astype(BF)
    out_ref[...] = (x1 + mm(ctx[...], w_out_ref[...])).astype(BF)


def body(
    volt,
    keep,
    site_ids,
    probe_ids,
    w_patch,
    site_table,
    probe_table,
    mask_token,
    gain_time,
    w_qkv_time,
    w_out_time,
    gain_cross,
    w_qkv_cross,
    w_out_cross,
):
    width = w_patch.shape[1]
    rows = volt[0, 0]
    count = rows.shape[0]
    mask = keep[0]
    steps = NX * NZ

    def shift(array, dx, dz):
        pairs = []
        for i in range(steps):
            x, z = divmod(i, NZ)
            pairs.append((i, ((x + dx) % NX) * NZ + (z + dz) % NZ))
        return lax.ppermute(array, "tm", pairs)

    def pack(cap):
        return call(
            pack_kernel,
            jax.ShapeDtypeStruct((cap, PACKED), BF),
            (mask, rows),
            scratch=(pltpu.VMEM((count, PACKED), BF),),
            vmem=4,
            flops=2 * cap * count * PACKED,
            nbytes=500_000,
        )

    packed = pack(CAP)
    tab, big, base = call(
        table_kernel,
        (
            jax.ShapeDtypeStruct((count, 2 * width), BF),
            jax.ShapeDtypeStruct((steps, width), F32),
            jax.ShapeDtypeStruct((8, width), F32),
        ),
        (site_ids, probe_ids, site_table, probe_table),
        smem=(0, 1),
        vmem=8,
        flops=2_000_000_000,
        nbytes=1_000_000,
    )
    shared = (w_patch, tab, big, base, gain_time, w_qkv_time)

    def own_part(after):
        return call(
            own_kernel,
            (
                jax.ShapeDtypeStruct((count, width), BF),
                jax.ShapeDtypeStruct((count, width), BF),
                jax.ShapeDtypeStruct((count, width), F32),
                jax.ShapeDtypeStruct((count, width), BF),
            ),
            (mask, rows, mask_token, *shared, after),
            vmem=24,
            flops=300_000_000,
            nbytes=100_000,
        )

    def attend(own, cap, vmem, mine=None):
        def group(blocks, offsets):
            return call(
                functools.partial(group_kernel, offsets, cap, len(blocks)),
                (
                    jax.ShapeDtypeStruct((len(offsets) * cap, 2 * width), BF),
                    jax.ShapeDtypeStruct((len(offsets), 128), F32),
                ),
                (*shared, *blocks),
                vmem=vmem,
                flops=2_500_000_000,
                nbytes=6_000_000,
            )

        below, above, beside = shift(own, 0, 1), shift(own, 0, -1), shift(own, 1, 0)
        first = group((own, below, above, beside), [(0, 0), (0, -1), (0, 1), (1, 0)])
        down2 = shift(jnp.concatenate([below, beside], axis=0), 0, 1)
        up2 = shift(jnp.concatenate([above, beside], axis=0), 0, -1)
        second = group((down2, up2), [(0, -2), (1, -1), (0, 2), (1, 1)])
        down3, up3 = shift(down2, 0, 1), shift(up2, 0, -1)
        third = group((down3, up3), [(0, -3), (1, -2), (0, 3), (1, 2)])
        down4 = shift(down3, 0, 1)
        far = shift(jnp.concatenate([up2[:cap], up3[:cap]], axis=0), 1, -1)
        mine = mine or own_part(third[1])
        x0, queries, own_scores, own_values = mine
        last = [(0, -4), (1, -3), (1, 3), (1, 4)]
        return mine, call(
            functools.partial(attend_kernel, last, cap, 3, 2),
            jax.ShapeDtypeStruct((count, width + 128), BF),
            (
                mask,
                *shared,
                queries,
                own_scores,
                own_values,
                x0,
                w_out_time,
                *first,
                *second,
                *third,
                down4,
                far,
            ),
            scratch=(pltpu.VMEM((steps * cap, 2 * width), BF), pltpu.VMEM((count, width), BF)),
            vmem=vmem + 8,
            flops=12_000_000_000,
            nbytes=10_000_000,
        )

    def trade(array):
        return lax.all_to_all(array, ("probe", "lane"), split_axis=0, concat_axis=0, tiled=True)

    def cross(window):
        return call(
            cross_kernel,
            (jax.ShapeDtypeStruct((count, width), BF), jax.ShapeDtypeStruct((1, 1), jnp.int32)),
            (window, gain_cross, w_qkv_cross, w_out_cross),
            smem_out=(1,),
            scratch=(pltpu.VMEM((count, width), BF),),
            flops=2_000_000_000,
            nbytes=6_000_000,
        )

    mine, x1 = attend(packed, CAP, 20)
    done, over = cross(trade(x1))
    general = over[0, 0] > 0

    def trade_by_pairs(array):
        parts = count // WIN
        here = lax.axis_index("probe") * lax.axis_size("lane") + lax.axis_index("lane")
        out = array
        for k in range(1, parts):
            there = (here ^ k) * WIN
            part = lax.dynamic_slice_in_dim(array, there, WIN, 0)
            part = lax.ppermute(part, ("probe", "lane"), [(i, i ^ k) for i in range(parts)])
            out = lax.dynamic_update_slice_in_dim(out, part, there, 0)
        return out

    def again():
        return trade_by_pairs(cross(trade_by_pairs(attend(pack(count), count, 50, mine)[1]))[0])

    out = trade(done)
    out = jnp.where(general, lax.cond(general, again, lambda: done), out)
    return out[None, None]


def solution(mesh):
    return jax.shard_map(
        body,
        mesh=mesh,
        in_specs=(
            P("probe", "lane", "tm", None),
            P("probe", "lane", "tm"),
            P("probe", "lane"),
            P("probe"),
            P(),
            P(),
            P(),
            P(),
            P(),
            P(),
            P(),
            P(),
            P(),
            P(),
        ),
        out_specs=P("probe", "lane", "tm", None),
        check_vma=False,
    )
```

```python
import functools
import math

import jax
import jax.numpy as jnp
from jax import lax
from jax.experimental import pallas as pl
from jax.experimental.pallas import tpu as pltpu
from jax.sharding import PartitionSpec as P

HEADS = 12
HEAD_DIM = 64
WIN = 16
PAIRS = HEADS // 2
PACKED = 512
COL_TIME, COL_VALID, COL_COUNT = 480, 481, 482
CAP = 96
NX, NZ = 2, 8
FAR = -1e30
BF = jnp.bfloat16
F32 = jnp.float32
NT = (((1,), (1,)), ((), ()))


def iota(shape, dim):
    return lax.broadcasted_iota(jnp.int32, shape, dim)


def mm(a, b):
    return jnp.dot(a, b, preferred_element_type=F32)


def norm(rows, gain):
    middle = jnp.mean(rows, axis=-1, keepdims=True)
    centred = rows - middle
    spread = jnp.mean(centred * centred, axis=-1, keepdims=True)
    return centred * lax.rsqrt(spread + 1e-05) * gain


def vector(ref):
    return ref[...].astype(F32).reshape(1, -1)


def split(value):
    high = value.astype(BF)
    return high, (value - high.astype(F32)).astype(BF)


def to_column(row):
    n = row.shape[1]
    eye = iota((n, n), 0) == iota((n, n), 1)
    return jnp.sum(jnp.where(eye, row, 0.0), axis=1, keepdims=True)


def call(kernel, out, args, *, smem=(), smem_out=(), scratch=(), vmem=16, flops=0, nbytes=0):
    several = isinstance(out, tuple)
    outs = out if several else (out,)


    def space(i, scalars):
        where = pltpu.SMEM if i in scalars else pltpu.VMEM
        return pl.BlockSpec(memory_space=where)

    specs = tuple(space(i, smem_out) for i in range(len(outs)))
    return pl.pallas_call(
        kernel,
        out_shape=out,
        in_specs=[space(i, smem) for i in range(len(args))],
        out_specs=specs if several else specs[0],
        scratch_shapes=list(scratch),
        compiler_params=pltpu.CompilerParams(vmem_limit_bytes=vmem * 1024 * 1024),
        cost_estimate=pl.CostEstimate(flops=flops, bytes_accessed=nbytes, transcendentals=0),
    )(*args)


def pack_kernel(keep_ref, volt_ref, out_ref, wide):
    count, samples = volt_ref.shape
    cap = out_ref.shape[0]
    lane = iota((count, PACKED), 1)
    extra = jnp.where(
        lane == COL_TIME, iota((count, PACKED), 0).astype(F32), jnp.where(lane == COL_VALID, 1.0, 0.0)
    )
    wide[...] = extra.astype(BF)
    mask = keep_ref[...].astype(F32)
    upper = jnp.where(iota((count, count), 0) <= iota((count, count), 1), 1.0, 0.0).astype(BF)
    rank = mm(jnp.broadcast_to(mask, (16, count)).astype(BF), upper)[0:1, :]
    pick = (rank - 1.0 == iota((cap, count), 0).astype(F32)) & (mask > 0.5)
    total = jnp.sum(mask, axis=1, keepdims=True)
    wide[:, :samples] = volt_ref[...]
    packed = mm(jnp.where(pick, 1.0, 0.0).astype(BF), wide[...])
    out_ref[...] = jnp.where(iota(packed.shape, 1) == COL_COUNT, total, packed).astype(BF)


def frequencies(rows, half):
    return jnp.exp(iota((rows, half), 1).astype(F32) * (-math.log(10000.0) / half))


def turn(at, by):
    return at[0] * by[1] + at[1] * by[0], at[1] * by[1] - at[0] * by[0]


def waves(rows, step, half):
    angle = (iota((rows, half), 0) * step).astype(F32) * frequencies(rows, half)
    return jnp.sin(angle), jnp.cos(angle)


def table_kernel(tab_ref, big_ref):
    count, width = tab_ref.shape[0], big_ref.shape[1]
    half = width // 2
    steps = big_ref.shape[0]
    big_ref[:, :half], big_ref[:, half:] = waves(steps, count, half)
    fine, middle = waves(16, 1, half), waves(count // 16, 16, half)
    for a in range(count // 16):
        at = slice(a * 16, (a + 1) * 16)
        row = [part[a : a + 1] for part in middle]
        for start, value in zip((0, half), turn(row, fine)):
            high, low = split(value)
            tab_ref[at, start : start + half] = high
            tab_ref[at, width + start : width + start + half] = low


def base_kernel(site_id_ref, probe_id_ref, site_ref, probe_ref, after_ref, base_ref):
    del after_ref
    sites, probes = site_ref.shape[0], probe_ref.shape[0]
    probe_id = probe_id_ref[...].reshape(1, 1)
    one_site = jnp.where(iota((16, sites), 1) == site_id_ref[...], 1.0, 0.0).astype(BF)
    one_probe = jnp.where(iota((16, probes), 1) == probe_id, 1.0, 0.0).astype(BF)
    base_ref[...] = mm(one_site, site_ref[...])[0:8] + mm(one_probe, probe_ref[...])[0:8]


def code_of(found, source, big_ref):
    width = big_ref.shape[1]
    half = width // 2
    local = found[:, :width] + found[:, width:]
    row = big_ref[pl.ds(source, 1), :]
    return jnp.concatenate(
        turn((row[:, :half], row[:, half:]), (local[:, :half], local[:, half:])), axis=1
    )


def own_kernel(
    keep_ref,
    volt_ref,
    token_ref,
    w_patch_ref,
    tab_ref,
    big_ref,
    base_ref,
    gain_ref,
    w_qkv_ref,
    after_ref,
    x0_ref,
    q_ref,
    self_ref,
    v_ref,
):
    del after_ref
    width = x0_ref.shape[1]
    code = code_of(tab_ref[...].astype(F32), lax.axis_index("tm"), big_ref)
    keep = to_column(keep_ref[...].astype(F32))
    proj = mm(volt_ref[...], w_patch_ref[...])
    proj = jnp.where(keep > 0.5, proj, vector(token_ref))
    x0 = (proj + base_ref[0:1, :] + code).astype(BF)
    x0_ref[...] = x0
    h1 = norm(x0.astype(F32), vector(gain_ref)).astype(BF)
    qkv = mm(h1, w_qkv_ref[...]).astype(BF)
    queries = (qkv[:, :width].astype(F32) * (1.0 / math.sqrt(HEAD_DIM))).astype(BF)
    q_ref[...] = queries
    v_ref[...] = qkv[:, 2 * width :]
    product = queries.astype(F32) * qkv[:, width : 2 * width].astype(F32)
    same_head = jnp.where(iota((128, 128), 0) // HEAD_DIM == iota((128, 128), 1) // HEAD_DIM, 1.0, 0.0).astype(BF)
    for pair in range(PAIRS):
        cols = slice(pair * 128, pair * 128 + 128)
        high, low = split(product[:, cols])
        score = mm(high, same_head) + mm(low, same_head)
        self_ref[:, cols] = jnp.where(keep > 0.5, FAR, score)


def keys_values(rows, offsets, cap, w_patch_ref, tab_ref, big_ref, base_ref, gain, w_qkv_ref):
    total = rows.shape[0]
    count, width = tab_ref.shape[0], base_ref.shape[1]
    samples = w_patch_ref.shape[0]
    local = rows[:, 384:512].astype(F32)[:, COL_TIME - 384 : COL_TIME - 383]
    proj = mm(rows[:, :samples], w_patch_ref[...])
    pick = jnp.where(iota((total, count), 1).astype(F32) == local, 1.0, 0.0).astype(BF)
    found = mm(pick, tab_ref[...])
    me = lax.axis_index("tm")
    x, z = me // NZ, lax.rem(me, NZ)
    code = []
    for i, (dx, dz) in enumerate(offsets):
        source = lax.rem(x + dx, NX) * NZ + lax.rem(z + dz + NZ, NZ)
        code.append(code_of(found[i * cap : (i + 1) * cap], source, big_ref))
    x0 = (proj + base_ref[0:1, :] + jnp.concatenate(code, axis=0)).astype(BF)
    h1 = norm(x0.astype(F32), gain).astype(BF)
    return mm(h1, w_qkv_ref[:, width:]).astype(BF)


def counts_of(rows, cap):
    heads = [rows[at : at + 1, COL_COUNT : COL_COUNT + 1] for at in range(0, rows.shape[0], cap)]
    return [head.astype(F32) for head in heads]


def cut(offsets, cap):
    each = max(1, 512 // cap)
    return [(at, offsets[at : at + each]) for at in range(0, len(offsets), each)]


def group_kernel(offsets, cap, nblocks, after, w_patch_ref, tab_ref, big_ref, base_ref, gain_ref, w_qkv_ref, *rest):
    blocks = rest[:nblocks]
    kv_ref, counts_ref = rest[nblocks + after :]
    rows = jnp.concatenate([block[...] for block in blocks], axis=0) if nblocks > 1 else blocks[0][...]
    for at, part in cut(offsets, cap):
        span = slice(at * cap, (at + len(part)) * cap)
        kv_ref[span, :] = keys_values(
            rows[span], part, cap, w_patch_ref, tab_ref, big_ref, base_ref, vector(gain_ref), w_qkv_ref
        )
    for i, number in enumerate(counts_of(rows, cap)):
        counts_ref[i : i + 1, :] = jnp.broadcast_to(number, (1, 128))


def attend_kernel(
    offsets,
    cap,
    ngroups,
    nblocks,
    keep_ref,
    w_patch_ref,
    tab_ref,
    big_ref,
    base_ref,
    gain_ref,
    w_qkv_ref,
    q_ref,
    self_ref,
    v_ref,
    x0_ref,
    w_out_ref,
    *rest,
):
    groups, rest = rest[: 2 * ngroups], rest[2 * ngroups :]
    blocks = rest[:nblocks]
    out_ref, kv, ctx = rest[nblocks:]
    count, width = x0_ref.shape
    rows = jnp.concatenate([block[...] for block in blocks], axis=0)
    counts, start = [], 0
    for kv_ref, counts_ref in zip(groups[::2], groups[1::2]):
        kv[start : start + kv_ref.shape[0], :] = kv_ref[...]
        start += kv_ref.shape[0]
        counts += [counts_ref[i : i + 1, 0:1] for i in range(counts_ref.shape[0])]
    for at, part in cut(offsets, cap):
        kv[start + at * cap : start + (at + len(part)) * cap, :] = keys_values(
            rows[at * cap : (at + len(part)) * cap],
            part,
            cap,
            w_patch_ref,
            tab_ref,
            big_ref,
            base_ref,
            vector(gain_ref),
            w_qkv_ref,
        )
    counts += counts_of(rows, cap)
    keys = kv.shape[0]
    place = iota((1, keys), 1)
    bias = jnp.full((1, keys), FAR, F32)
    most = counts[0]
    for i, number in enumerate(counts):
        inside = (place >= i * cap) & ((place - i * cap).astype(F32) < jnp.minimum(number, cap))
        bias = jnp.where(inside, 0.0, bias)
        most = jnp.maximum(most, number)

    low = iota((count, 128), 1) < HEAD_DIM
    ones = jnp.ones((keys, 128), BF)

    def one_pair(pair):
        at = pair * 128 if isinstance(pair, int) else pl.multiple_of(pair * 128, 128)
        cols, value_cols = pl.ds(at, 128), pl.ds(width + at, 128)
        queries = q_ref[:, cols]
        zero = jnp.zeros_like(queries)
        both = jnp.concatenate([jnp.where(low, queries, zero), jnp.where(low, zero, queries)], axis=0)
        scores = lax.dot_general(both, kv[:, cols], NT, preferred_element_type=F32) + bias
        own = self_ref[:, cols]
        own = jnp.concatenate([own[:, 0:1], own[:, HEAD_DIM : HEAD_DIM + 1]], axis=0)
        top = jnp.maximum(jnp.max(scores, axis=1, keepdims=True), own)
        weights = jnp.exp(scores - top).astype(BF)
        mixed = mm(weights, jnp.concatenate([kv[:, value_cols], ones], axis=1))
        own = jnp.exp(own - top)
        total = mixed[:, 128:] + own
        own = own.astype(BF).astype(F32)
        values = v_ref[:, cols].astype(F32)
        first = (mixed[:count, :128] + own[:count] * values) / total[:count]
        second = (mixed[count:, :128] + own[count:] * values) / total[count:]
        ctx[:, cols] = jnp.where(low, first, second).astype(BF)

    if keys <= 2048:
        for pair in range(PAIRS):
            one_pair(pair)
    else:
        pl.loop(0, PAIRS)(one_pair)
    x1 = x0_ref[...].astype(F32) + mm(ctx[...], w_out_ref[...])
    out_ref[:, :width] = x1.astype(BF)
    keep = to_column(keep_ref[...].astype(F32))
    over = jnp.where(most > cap, 1.0, 0.0)
    out_ref[:, width:] = jnp.where(iota((count, 128), 1) == 0, keep, over).astype(BF)


def cross_kernel(x_ref, gain_ref, w_qkv_ref, w_out_ref, out_ref, over_ref, ctx):
    count, width = out_ref.shape
    over_ref[0, 0] = jnp.max(x_ref[:, width:].astype(F32)[:, 1:2]).astype(jnp.int32)
    x1 = x_ref[:, :width].astype(F32)
    h2 = norm(x1, vector(gain_ref)).astype(BF)
    qkv = mm(h2, w_qkv_ref[...]).astype(BF)
    seen = x_ref[:, width:].astype(F32)[:, 0:1]
    eye = iota((count, count), 0) == iota((count, count), 1)
    seen = jnp.sum(jnp.where(eye, seen, 0.0), axis=0, keepdims=True)
    bias = jnp.where(eye | (seen > 0.5), 0.0, FAR)
    bias = jnp.concatenate([bias, bias], axis=0)
    lane = iota((count, 128), 1)
    low = lane < HEAD_DIM
    scale = 1.0 / math.sqrt(HEAD_DIM)
    ones = jnp.ones((count, 128), BF)
    for pair in range(PAIRS):
        at = pair * 128
        queries = (qkv[:, at : at + 128].astype(F32) * scale).astype(BF)
        zero = jnp.zeros_like(queries)
        both = jnp.concatenate([jnp.where(low, queries, zero), jnp.where(low, zero, queries)], axis=0)
        scores = lax.dot_general(both, qkv[:, width + at : width + at + 128], NT, preferred_element_type=F32)
        scores = scores + bias
        top = jnp.max(scores, axis=1, keepdims=True)
        weights = jnp.exp(scores - top).astype(BF)
        values = jnp.concatenate([qkv[:, 2 * width + at : 2 * width + at + 128], ones], axis=1)
        mixed = mm(weights, values)
        done = mixed[:, :128] / mixed[:, 128:]
        ctx[:, at : at + 128] = jnp.where(low, done[:count], done[count:]).astype(BF)
    out_ref[...] = (x1 + mm(ctx[...], w_out_ref[...])).astype(BF)


def body(
    volt,
    keep,
    site_ids,
    probe_ids,
    w_patch,
    site_table,
    probe_table,
    mask_token,
    gain_time,
    w_qkv_time,
    w_out_time,
    gain_cross,
    w_qkv_cross,
    w_out_cross,
):
    width = w_patch.shape[1]
    rows = volt[0, 0]
    count = rows.shape[0]
    mask = keep[0]
    steps = NX * NZ

    def shift(array, dx, dz):
        pairs = []
        for i in range(steps):
            x, z = divmod(i, NZ)
            pairs.append((i, ((x + dx) % NX) * NZ + (z + dz) % NZ))
        return lax.ppermute(array, "tm", pairs)

    def pack(cap):
        return call(
            pack_kernel,
            jax.ShapeDtypeStruct((cap, PACKED), BF),
            (mask, rows),
            scratch=(pltpu.VMEM((count, PACKED), BF),),
            vmem=4,
            flops=2 * cap * count * PACKED,
            nbytes=500_000,
        )

    packed = pack(CAP)
    tab, big = call(
        table_kernel,
        (jax.ShapeDtypeStruct((count, 2 * width), BF), jax.ShapeDtypeStruct((steps, width), F32)),
        (),
        vmem=8,
        flops=2_000_000_000,
        nbytes=1_000_000,
    )
    base = call(
        base_kernel,
        jax.ShapeDtypeStruct((8, width), F32),
        (site_ids, probe_ids, site_table, probe_table, big),
        vmem=4,
        flops=10_000_000,
        nbytes=200_000,
    )
    shared = (w_patch, tab, big, base, gain_time, w_qkv_time)

    def own_part(after):
        return call(
            own_kernel,
            (
                jax.ShapeDtypeStruct((count, width), BF),
                jax.ShapeDtypeStruct((count, width), BF),
                jax.ShapeDtypeStruct((count, width), F32),
                jax.ShapeDtypeStruct((count, width), BF),
            ),
            (mask, rows, mask_token, *shared, after),
            vmem=24,
            flops=300_000_000,
            nbytes=100_000,
        )

    def attend(own, cap, vmem, mine=None):
        def group(blocks, offsets, after=()):
            return call(
                functools.partial(group_kernel, offsets, cap, len(blocks), len(after)),
                (
                    jax.ShapeDtypeStruct((len(offsets) * cap, 2 * width), BF),
                    jax.ShapeDtypeStruct((len(offsets), 128), F32),
                ),
                (*shared, *blocks, *after),
                vmem=vmem,
                flops=2_500_000_000,
                nbytes=6_000_000,
            )

        below, above, beside = shift(own, 0, 1), shift(own, 0, -1), shift(own, 1, 0)
        first = group((own, below, above, beside), [(0, 0), (0, -1), (0, 1), (1, 0)])
        down2 = shift(jnp.concatenate([below, beside], axis=0), 0, 1)
        up2 = shift(jnp.concatenate([above, beside], axis=0), 0, -1)
        mine = mine or own_part(first[1])
        x0, queries, own_scores, own_values = mine
        second = group((down2, up2), [(0, -2), (1, -1), (0, 2), (1, 1)], (x0,))
        down3, up3 = shift(down2, 0, 1), shift(up2, 0, -1)
        third = group((down3, up3), [(0, -3), (1, -2), (0, 3), (1, 2)])
        down4 = shift(down3, 0, 1)
        far = shift(jnp.concatenate([up2[:cap], up3[:cap]], axis=0), 1, -1)
        last = [(0, -4), (1, -3), (1, 3), (1, 4)]
        return mine, call(
            functools.partial(attend_kernel, last, cap, 3, 2),
            jax.ShapeDtypeStruct((count, width + 128), BF),
            (
                mask,
                *shared,
                queries,
                own_scores,
                own_values,
                x0,
                w_out_time,
                *first,
                *second,
                *third,
                down4,
                far,
            ),
            scratch=(pltpu.VMEM((steps * cap, 2 * width), BF), pltpu.VMEM((count, width), BF)),
            vmem=vmem + 8,
            flops=12_000_000_000,
            nbytes=10_000_000,
        )

    def trade(array):
        return lax.all_to_all(array, ("probe", "lane"), split_axis=0, concat_axis=0, tiled=True)

    def cross(window):
        return call(
            cross_kernel,
            (jax.ShapeDtypeStruct((count, width), BF), jax.ShapeDtypeStruct((1, 1), jnp.int32)),
            (window, gain_cross, w_qkv_cross, w_out_cross),
            smem_out=(1,),
            scratch=(pltpu.VMEM((count, width), BF),),
            flops=2_000_000_000,
            nbytes=6_000_000,
        )

    mine, x1 = attend(packed, CAP, 20)
    done, over = cross(trade(x1))
    general = over[0, 0] > 0

    def trade_by_pairs(array):
        parts = count // WIN
        here = lax.axis_index("probe") * lax.axis_size("lane") + lax.axis_index("lane")
        out = array
        for k in range(1, parts):
            there = (here ^ k) * WIN
            part = lax.dynamic_slice_in_dim(array, there, WIN, 0)
            part = lax.ppermute(part, ("probe", "lane"), [(i, i ^ k) for i in range(parts)])
            out = lax.dynamic_update_slice_in_dim(out, part, there, 0)
        return out

    def again():
        return trade_by_pairs(cross(trade_by_pairs(attend(pack(count), count, 50, mine)[1]))[0])

    out = trade(done)
    out = jnp.where(general, lax.cond(general, again, lambda: done), out)
    return out[None, None]


def solution(mesh):
    return jax.shard_map(
        body,
        mesh=mesh,
        in_specs=(
            P("probe", "lane", "tm", None),
            P("probe", "lane", "tm"),
            P("probe", "lane"),
            P("probe"),
            P(),
            P(),
            P(),
            P(),
            P(),
            P(),
            P(),
            P(),
            P(),
            P(),
        ),
        out_specs=P("probe", "lane", "tm", None),
        check_vma=False,
    )
```

```python
import functools
import math

import jax
import jax.numpy as jnp
from jax import lax
from jax.experimental import pallas as pl
from jax.experimental.pallas import tpu as pltpu
from jax.sharding import PartitionSpec as P

HEADS = 12
HEAD_DIM = 64
WIN = 16
PAIRS = HEADS // 2
PACKED = 512
COL_TIME, COL_VALID, COL_COUNT = 480, 481, 482
CAP = 96
NX, NZ = 2, 8
FAR = -1e30
BF = jnp.bfloat16
F32 = jnp.float32
NT = (((1,), (1,)), ((), ()))


def iota(shape, dim):
    return lax.broadcasted_iota(jnp.int32, shape, dim)


def mm(a, b):
    return jnp.dot(a, b, preferred_element_type=F32)


def norm(rows, gain):
    middle = jnp.mean(rows, axis=-1, keepdims=True)
    centred = rows - middle
    spread = jnp.mean(centred * centred, axis=-1, keepdims=True)
    return centred * lax.rsqrt(spread + 1e-05) * gain


def vector(ref):
    return ref[...].astype(F32).reshape(1, -1)


def split(value):
    high = value.astype(BF)
    return high, (value - high.astype(F32)).astype(BF)


def to_column(row):
    n = row.shape[1]
    eye = iota((n, n), 0) == iota((n, n), 1)
    return jnp.sum(jnp.where(eye, row, 0.0), axis=1, keepdims=True)


def call(kernel, out, args, *, smem=(), smem_out=(), scratch=(), vmem=16, flops=0, nbytes=0):
    several = isinstance(out, tuple)
    outs = out if several else (out,)


    def space(i, scalars):
        where = pltpu.SMEM if i in scalars else pltpu.VMEM
        return pl.BlockSpec(memory_space=where)

    specs = tuple(space(i, smem_out) for i in range(len(outs)))
    return pl.pallas_call(
        kernel,
        out_shape=out,
        in_specs=[space(i, smem) for i in range(len(args))],
        out_specs=specs if several else specs[0],
        scratch_shapes=list(scratch),
        compiler_params=pltpu.CompilerParams(vmem_limit_bytes=vmem * 1024 * 1024),
        cost_estimate=pl.CostEstimate(flops=flops, bytes_accessed=nbytes, transcendentals=0),
    )(*args)


def pack_kernel(keep_ref, volt_ref, out_ref, wide):
    count, samples = volt_ref.shape
    cap = out_ref.shape[0]
    lane = iota((count, PACKED), 1)
    extra = jnp.where(
        lane == COL_TIME, iota((count, PACKED), 0).astype(F32), jnp.where(lane == COL_VALID, 1.0, 0.0)
    )
    wide[...] = extra.astype(BF)
    mask = keep_ref[...].astype(F32)
    upper = jnp.where(iota((count, count), 0) <= iota((count, count), 1), 1.0, 0.0).astype(BF)
    rank = mm(jnp.broadcast_to(mask, (16, count)).astype(BF), upper)[0:1, :]
    pick = (rank - 1.0 == iota((cap, count), 0).astype(F32)) & (mask > 0.5)
    total = jnp.sum(mask, axis=1, keepdims=True)
    wide[:, :samples] = volt_ref[...]
    packed = mm(jnp.where(pick, 1.0, 0.0).astype(BF), wide[...])
    out_ref[...] = jnp.where(iota(packed.shape, 1) == COL_COUNT, total, packed).astype(BF)


def frequencies(rows, half):
    return jnp.exp(iota((rows, half), 1).astype(F32) * (-math.log(10000.0) / half))


def turn(at, by):
    return at[0] * by[1] + at[1] * by[0], at[1] * by[1] - at[0] * by[0]


def waves(rows, step, half):
    angle = (iota((rows, half), 0) * step).astype(F32) * frequencies(rows, half)
    return jnp.sin(angle), jnp.cos(angle)


def table_kernel(tab_ref, big_ref):
    count, width = tab_ref.shape[0], big_ref.shape[1]
    half = width // 2
    steps = big_ref.shape[0]
    big_ref[:, :half], big_ref[:, half:] = waves(steps, count, half)
    fine, middle = waves(16, 1, half), waves(count // 16, 16, half)
    for a in range(count // 16):
        at = slice(a * 16, (a + 1) * 16)
        row = [part[a : a + 1] for part in middle]
        for start, value in zip((0, half), turn(row, fine)):
            high, low = split(value)
            tab_ref[at, start : start + half] = high
            tab_ref[at, width + start : width + start + half] = low


def base_kernel(site_id_ref, probe_id_ref, site_ref, probe_ref, after_ref, base_ref):
    del after_ref
    sites, probes = site_ref.shape[0], probe_ref.shape[0]
    probe_id = probe_id_ref[...].reshape(1, 1)
    one_site = jnp.where(iota((16, sites), 1) == site_id_ref[...], 1.0, 0.0).astype(BF)
    one_probe = jnp.where(iota((16, probes), 1) == probe_id, 1.0, 0.0).astype(BF)
    base_ref[...] = mm(one_site, site_ref[...])[0:8] + mm(one_probe, probe_ref[...])[0:8]


def code_of(found, source, big_ref):
    width = big_ref.shape[1]
    half = width // 2
    local = found[:, :width] + found[:, width:]
    row = big_ref[pl.ds(source, 1), :]
    return jnp.concatenate(
        turn((row[:, :half], row[:, half:]), (local[:, :half], local[:, half:])), axis=1
    )


def own_kernel(
    keep_ref,
    volt_ref,
    token_ref,
    w_patch_ref,
    tab_ref,
    big_ref,
    base_ref,
    gain_ref,
    w_qkv_ref,
    after_ref,
    x0_ref,
    q_ref,
    self_ref,
    v_ref,
):
    del after_ref
    width = x0_ref.shape[1]
    code = code_of(tab_ref[...].astype(F32), lax.axis_index("tm"), big_ref)
    keep = to_column(keep_ref[...].astype(F32))
    proj = mm(volt_ref[...], w_patch_ref[...])
    proj = jnp.where(keep > 0.5, proj, vector(token_ref))
    x0 = (proj + base_ref[0:1, :] + code).astype(BF)
    x0_ref[...] = x0
    h1 = norm(x0.astype(F32), vector(gain_ref)).astype(BF)
    qkv = mm(h1, w_qkv_ref[...]).astype(BF)
    queries = (qkv[:, :width].astype(F32) * (1.0 / math.sqrt(HEAD_DIM))).astype(BF)
    q_ref[...] = queries
    v_ref[...] = qkv[:, 2 * width :]
    product = queries.astype(F32) * qkv[:, width : 2 * width].astype(F32)
    same_head = jnp.where(iota((128, 128), 0) // HEAD_DIM == iota((128, 128), 1) // HEAD_DIM, 1.0, 0.0).astype(BF)
    for pair in range(PAIRS):
        cols = slice(pair * 128, pair * 128 + 128)
        high, low = split(product[:, cols])
        score = mm(high, same_head) + mm(low, same_head)
        self_ref[:, cols] = jnp.where(keep > 0.5, FAR, score)


def keys_values(rows, offsets, cap, w_patch_ref, tab_ref, big_ref, base_ref, gain, w_qkv_ref):
    total = rows.shape[0]
    count, width = tab_ref.shape[0], base_ref.shape[1]
    samples = w_patch_ref.shape[0]
    local = rows[:, 384:512].astype(F32)[:, COL_TIME - 384 : COL_TIME - 383]
    proj = mm(rows[:, :samples], w_patch_ref[...])
    pick = jnp.where(iota((total, count), 1).astype(F32) == local, 1.0, 0.0).astype(BF)
    found = mm(pick, tab_ref[...])
    me = lax.axis_index("tm")
    x, z = me // NZ, lax.rem(me, NZ)
    code = []
    for i, (dx, dz) in enumerate(offsets):
        source = lax.rem(x + dx, NX) * NZ + lax.rem(z + dz + NZ, NZ)
        code.append(code_of(found[i * cap : (i + 1) * cap], source, big_ref))
    x0 = (proj + base_ref[0:1, :] + jnp.concatenate(code, axis=0)).astype(BF)
    h1 = norm(x0.astype(F32), gain).astype(BF)
    return mm(h1, w_qkv_ref[:, width:]).astype(BF)


def counts_of(rows, cap):
    heads = [rows[at : at + 1, COL_COUNT : COL_COUNT + 1] for at in range(0, rows.shape[0], cap)]
    return [head.astype(F32) for head in heads]


def cut(offsets, cap):
    each = max(1, 512 // cap)
    return [(at, offsets[at : at + each]) for at in range(0, len(offsets), each)]


def group_kernel(offsets, cap, nblocks, after, w_patch_ref, tab_ref, big_ref, base_ref, gain_ref, w_qkv_ref, *rest):
    blocks = rest[:nblocks]
    kv_ref, counts_ref = rest[nblocks + after :]
    rows = jnp.concatenate([block[...] for block in blocks], axis=0) if nblocks > 1 else blocks[0][...]
    for at, part in cut(offsets, cap):
        span = slice(at * cap, (at + len(part)) * cap)
        kv_ref[span, :] = keys_values(
            rows[span], part, cap, w_patch_ref, tab_ref, big_ref, base_ref, vector(gain_ref), w_qkv_ref
        )
    for i, number in enumerate(counts_of(rows, cap)):
        counts_ref[i : i + 1, :] = jnp.broadcast_to(number, (1, 128))


def both_heads(queries):
    low = iota(queries.shape, 1) < HEAD_DIM
    zero = jnp.zeros_like(queries)
    return jnp.concatenate([jnp.where(low, queries, zero), jnp.where(low, zero, queries)], axis=0)


def score_kernel(q_ref, *rest):
    groups, out_ref = rest[:-1], rest[-1]
    for pair in range(PAIRS):
        cols = slice(pair * 128, pair * 128 + 128)
        keys = jnp.concatenate([kv_ref[:, cols] for kv_ref in groups], axis=0)
        out_ref[pair] = lax.dot_general(both_heads(q_ref[:, cols]), keys, NT, preferred_element_type=F32)


def attend_kernel(
    offsets,
    cap,
    ngroups,
    nblocks,
    nearly,
    keep_ref,
    w_patch_ref,
    tab_ref,
    big_ref,
    base_ref,
    gain_ref,
    w_qkv_ref,
    q_ref,
    self_ref,
    v_ref,
    x0_ref,
    w_out_ref,
    *rest,
):
    groups, rest = rest[: 2 * ngroups], rest[2 * ngroups :]
    blocks, early = rest[:nblocks], rest[nblocks : nblocks + nearly]
    out_ref, kv, ctx = rest[nblocks + nearly :]
    count, width = x0_ref.shape
    rows = jnp.concatenate([block[...] for block in blocks], axis=0)
    counts, start = [], 0
    for kv_ref, counts_ref in zip(groups[::2], groups[1::2]):
        skip = width if early else 0
        kv[start : start + kv_ref.shape[0], skip:] = kv_ref[:, skip:]
        start += kv_ref.shape[0]
        counts += [counts_ref[i : i + 1, 0:1] for i in range(counts_ref.shape[0])]
    for at, part in cut(offsets, cap):
        kv[start + at * cap : start + (at + len(part)) * cap, :] = keys_values(
            rows[at * cap : (at + len(part)) * cap],
            part,
            cap,
            w_patch_ref,
            tab_ref,
            big_ref,
            base_ref,
            vector(gain_ref),
            w_qkv_ref,
        )
    counts += counts_of(rows, cap)
    keys = kv.shape[0]
    place = iota((1, keys), 1)
    bias = jnp.full((1, keys), FAR, F32)
    most = counts[0]
    for i, number in enumerate(counts):
        inside = (place >= i * cap) & ((place - i * cap).astype(F32) < jnp.minimum(number, cap))
        bias = jnp.where(inside, 0.0, bias)
        most = jnp.maximum(most, number)

    low = iota((count, 128), 1) < HEAD_DIM
    ones = jnp.ones((keys, 128), BF)

    def one_pair(pair):
        at = pair * 128 if isinstance(pair, int) else pl.multiple_of(pair * 128, 128)
        cols, value_cols = pl.ds(at, 128), pl.ds(width + at, 128)
        both = both_heads(q_ref[:, cols])
        keys_here = kv[start:, cols] if early else kv[:, cols]
        scores = lax.dot_general(both, keys_here, NT, preferred_element_type=F32)
        if early:
            scores = jnp.concatenate([early[0][pair], scores], axis=1)
        scores = scores + bias
        own = self_ref[:, cols]
        own = jnp.concatenate([own[:, 0:1], own[:, HEAD_DIM : HEAD_DIM + 1]], axis=0)
        top = jnp.maximum(jnp.max(scores, axis=1, keepdims=True), own)
        weights = jnp.exp(scores - top).astype(BF)
        mixed = mm(weights, jnp.concatenate([kv[:, value_cols], ones], axis=1))
        own = jnp.exp(own - top)
        total = mixed[:, 128:] + own
        own = own.astype(BF).astype(F32)
        values = v_ref[:, cols].astype(F32)
        first = (mixed[:count, :128] + own[:count] * values) / total[:count]
        second = (mixed[count:, :128] + own[count:] * values) / total[count:]
        ctx[:, cols] = jnp.where(low, first, second).astype(BF)

    if keys <= 2048:
        for pair in range(PAIRS):
            one_pair(pair)
    else:
        pl.loop(0, PAIRS)(one_pair)
    x1 = x0_ref[...].astype(F32) + mm(ctx[...], w_out_ref[...])
    out_ref[:, :width] = x1.astype(BF)
    keep = to_column(keep_ref[...].astype(F32))
    over = jnp.where(most > cap, 1.0, 0.0)
    out_ref[:, width:] = jnp.where(iota((count, 128), 1) == 0, keep, over).astype(BF)


def cross_kernel(x_ref, gain_ref, w_qkv_ref, w_out_ref, out_ref, over_ref, ctx):
    count, width = out_ref.shape
    over_ref[0, 0] = jnp.max(x_ref[:, width:].astype(F32)[:, 1:2]).astype(jnp.int32)
    x1 = x_ref[:, :width].astype(F32)
    h2 = norm(x1, vector(gain_ref)).astype(BF)
    qkv = mm(h2, w_qkv_ref[...]).astype(BF)
    seen = x_ref[:, width:].astype(F32)[:, 0:1]
    eye = iota((count, count), 0) == iota((count, count), 1)
    seen = jnp.sum(jnp.where(eye, seen, 0.0), axis=0, keepdims=True)
    bias = jnp.where(eye | (seen > 0.5), 0.0, FAR)
    bias = jnp.concatenate([bias, bias], axis=0)
    lane = iota((count, 128), 1)
    low = lane < HEAD_DIM
    scale = 1.0 / math.sqrt(HEAD_DIM)
    ones = jnp.ones((count, 128), BF)
    for pair in range(PAIRS):
        at = pair * 128
        both = both_heads((qkv[:, at : at + 128].astype(F32) * scale).astype(BF))
        scores = lax.dot_general(both, qkv[:, width + at : width + at + 128], NT, preferred_element_type=F32)
        scores = scores + bias
        top = jnp.max(scores, axis=1, keepdims=True)
        weights = jnp.exp(scores - top).astype(BF)
        values = jnp.concatenate([qkv[:, 2 * width + at : 2 * width + at + 128], ones], axis=1)
        mixed = mm(weights, values)
        done = mixed[:, :128] / mixed[:, 128:]
        ctx[:, at : at + 128] = jnp.where(low, done[:count], done[count:]).astype(BF)
    out_ref[...] = (x1 + mm(ctx[...], w_out_ref[...])).astype(BF)


def body(
    volt,
    keep,
    site_ids,
    probe_ids,
    w_patch,
    site_table,
    probe_table,
    mask_token,
    gain_time,
    w_qkv_time,
    w_out_time,
    gain_cross,
    w_qkv_cross,
    w_out_cross,
):
    width = w_patch.shape[1]
    rows = volt[0, 0]
    count = rows.shape[0]
    mask = keep[0]
    steps = NX * NZ

    def shift(array, dx, dz):
        pairs = []
        for i in range(steps):
            x, z = divmod(i, NZ)
            pairs.append((i, ((x + dx) % NX) * NZ + (z + dz) % NZ))
        return lax.ppermute(array, "tm", pairs)

    def pack(cap):
        return call(
            pack_kernel,
            jax.ShapeDtypeStruct((cap, PACKED), BF),
            (mask, rows),
            scratch=(pltpu.VMEM((count, PACKED), BF),),
            vmem=4,
            flops=2 * cap * count * PACKED,
            nbytes=500_000,
        )

    packed = pack(CAP)
    tab, big = call(
        table_kernel,
        (jax.ShapeDtypeStruct((count, 2 * width), BF), jax.ShapeDtypeStruct((steps, width), F32)),
        (),
        vmem=8,
        flops=2_000_000_000,
        nbytes=1_000_000,
    )
    base = call(
        base_kernel,
        jax.ShapeDtypeStruct((8, width), F32),
        (site_ids, probe_ids, site_table, probe_table, big),
        vmem=4,
        flops=10_000_000,
        nbytes=200_000,
    )
    shared = (w_patch, tab, big, base, gain_time, w_qkv_time)

    def own_part(after):
        return call(
            own_kernel,
            (
                jax.ShapeDtypeStruct((count, width), BF),
                jax.ShapeDtypeStruct((count, width), BF),
                jax.ShapeDtypeStruct((count, width), F32),
                jax.ShapeDtypeStruct((count, width), BF),
            ),
            (mask, rows, mask_token, *shared, after),
            vmem=24,
            flops=300_000_000,
            nbytes=100_000,
        )

    def attend(own, cap, vmem, mine=None):
        def group(blocks, offsets, after=()):
            return call(
                functools.partial(group_kernel, offsets, cap, len(blocks), len(after)),
                (
                    jax.ShapeDtypeStruct((len(offsets) * cap, 2 * width), BF),
                    jax.ShapeDtypeStruct((len(offsets), 128), F32),
                ),
                (*shared, *blocks, *after),
                vmem=vmem,
                flops=2_500_000_000,
                nbytes=6_000_000,
            )

        below, above, beside = shift(own, 0, 1), shift(own, 0, -1), shift(own, 1, 0)
        first = group((own, below, above, beside), [(0, 0), (0, -1), (0, 1), (1, 0)])
        down2 = shift(jnp.concatenate([below, beside], axis=0), 0, 1)
        up2 = shift(jnp.concatenate([above, beside], axis=0), 0, -1)
        mine = mine or own_part(first[1])
        x0, queries, own_scores, own_values = mine
        second = group((down2, up2), [(0, -2), (1, -1), (0, 2), (1, 1)], (x0,))
        down3, up3 = shift(down2, 0, 1), shift(up2, 0, -1)
        third = group((down3, up3), [(0, -3), (1, -2), (0, 3), (1, 2)])
        down4 = shift(down3, 0, 1)
        far = shift(jnp.concatenate([up2[:cap], up3[:cap]], axis=0), 1, -1)
        early = ()
        if cap <= CAP:
            groups = (first[0], second[0], third[0])
            keys = sum(group.shape[0] for group in groups)
            early = (
                call(
                    score_kernel,
                    jax.ShapeDtypeStruct((PAIRS, 2 * count, keys), F32),
                    (queries, *groups),
                    vmem=8,
                    flops=300_000_000,
                    nbytes=100_000,
                ),
            )
        last = [(0, -4), (1, -3), (1, 3), (1, 4)]
        return mine, call(
            functools.partial(attend_kernel, last, cap, 3, 2, len(early)),
            jax.ShapeDtypeStruct((count, width + 128), BF),
            (
                mask,
                *shared,
                queries,
                own_scores,
                own_values,
                x0,
                w_out_time,
                *first,
                *second,
                *third,
                down4,
                far,
                *early,
            ),
            scratch=(pltpu.VMEM((steps * cap, 2 * width), BF), pltpu.VMEM((count, width), BF)),
            vmem=vmem + 8,
            flops=12_000_000_000,
            nbytes=10_000_000,
        )

    def trade(array):
        return lax.all_to_all(array, ("probe", "lane"), split_axis=0, concat_axis=0, tiled=True)

    def cross(window):
        return call(
            cross_kernel,
            (jax.ShapeDtypeStruct((count, width), BF), jax.ShapeDtypeStruct((1, 1), jnp.int32)),
            (window, gain_cross, w_qkv_cross, w_out_cross),
            smem_out=(1,),
            scratch=(pltpu.VMEM((count, width), BF),),
            flops=2_000_000_000,
            nbytes=6_000_000,
        )

    mine, x1 = attend(packed, CAP, 20)
    done, over = cross(trade(x1))
    general = over[0, 0] > 0

    def trade_by_pairs(array):
        parts = count // WIN
        here = lax.axis_index("probe") * lax.axis_size("lane") + lax.axis_index("lane")
        out = array
        for k in range(1, parts):
            there = (here ^ k) * WIN
            part = lax.dynamic_slice_in_dim(array, there, WIN, 0)
            part = lax.ppermute(part, ("probe", "lane"), [(i, i ^ k) for i in range(parts)])
            out = lax.dynamic_update_slice_in_dim(out, part, there, 0)
        return out

    def again():
        return trade_by_pairs(cross(trade_by_pairs(attend(pack(count), count, 50, mine)[1]))[0])

    out = trade(done)
    out = jnp.where(general, lax.cond(general, again, lambda: done), out)
    return out[None, None]


def solution(mesh):
    return jax.shard_map(
        body,
        mesh=mesh,
        in_specs=(
            P("probe", "lane", "tm", None),
            P("probe", "lane", "tm"),
            P("probe", "lane"),
            P("probe"),
            P(),
            P(),
            P(),
            P(),
            P(),
            P(),
            P(),
            P(),
            P(),
            P(),
        ),
        out_specs=P("probe", "lane", "tm", None),
        check_vma=False,
    )
```

```python
import functools
import math

import jax
import jax.numpy as jnp
from jax import lax
from jax.experimental import pallas as pl
from jax.experimental.pallas import tpu as pltpu
from jax.sharding import PartitionSpec as P

HEADS = 12
HEAD_DIM = 64
WIN = 16
PAIRS = HEADS // 2
PACKED = 512
COL_TIME, COL_VALID, COL_COUNT = 480, 481, 482
CAP = 96
NX, NZ = 2, 8
FAR = -1e30
BF = jnp.bfloat16
F32 = jnp.float32
NT = (((1,), (1,)), ((), ()))


def iota(shape, dim):
    return lax.broadcasted_iota(jnp.int32, shape, dim)


def mm(a, b):
    return jnp.dot(a, b, preferred_element_type=F32)


def norm(rows, gain):
    middle = jnp.mean(rows, axis=-1, keepdims=True)
    centred = rows - middle
    spread = jnp.mean(centred * centred, axis=-1, keepdims=True)
    return centred * lax.rsqrt(spread + 1e-05) * gain


def vector(ref):
    return ref[...].astype(F32).reshape(1, -1)


def split(value):
    high = value.astype(BF)
    return high, (value - high.astype(F32)).astype(BF)


def to_column(row):
    n = row.shape[1]
    eye = iota((n, n), 0) == iota((n, n), 1)
    return jnp.sum(jnp.where(eye, row, 0.0), axis=1, keepdims=True)


def call(kernel, out, args, *, smem=(), smem_out=(), scratch=(), vmem=16, flops=0, nbytes=0):
    several = isinstance(out, tuple)
    outs = out if several else (out,)


    def space(i, scalars):
        where = pltpu.SMEM if i in scalars else pltpu.VMEM
        return pl.BlockSpec(memory_space=where)

    specs = tuple(space(i, smem_out) for i in range(len(outs)))
    return pl.pallas_call(
        kernel,
        out_shape=out,
        in_specs=[space(i, smem) for i in range(len(args))],
        out_specs=specs if several else specs[0],
        scratch_shapes=list(scratch),
        compiler_params=pltpu.CompilerParams(vmem_limit_bytes=vmem * 1024 * 1024),
        cost_estimate=pl.CostEstimate(flops=flops, bytes_accessed=nbytes, transcendentals=0),
    )(*args)


def pack_kernel(keep_ref, volt_ref, out_ref, wide):
    count, samples = volt_ref.shape
    cap = out_ref.shape[0]
    lane = iota((count, PACKED), 1)
    extra = jnp.where(
        lane == COL_TIME, iota((count, PACKED), 0).astype(F32), jnp.where(lane == COL_VALID, 1.0, 0.0)
    )
    wide[...] = extra.astype(BF)
    mask = keep_ref[...].astype(F32)
    upper = jnp.where(iota((count, count), 0) <= iota((count, count), 1), 1.0, 0.0).astype(BF)
    rank = mm(jnp.broadcast_to(mask, (16, count)).astype(BF), upper)[0:1, :]
    pick = (rank - 1.0 == iota((cap, count), 0).astype(F32)) & (mask > 0.5)
    total = jnp.sum(mask, axis=1, keepdims=True)
    wide[:, :samples] = volt_ref[...]
    packed = mm(jnp.where(pick, 1.0, 0.0).astype(BF), wide[...])
    out_ref[...] = jnp.where(iota(packed.shape, 1) == COL_COUNT, total, packed).astype(BF)


def frequencies(rows, half):
    return jnp.exp(iota((rows, half), 1).astype(F32) * (-math.log(10000.0) / half))


def turn(at, by):
    return at[0] * by[1] + at[1] * by[0], at[1] * by[1] - at[0] * by[0]


def waves(rows, step, half):
    angle = (iota((rows, half), 0) * step).astype(F32) * frequencies(rows, half)
    return jnp.sin(angle), jnp.cos(angle)


def table_kernel(tab_ref, big_ref):
    count, width = tab_ref.shape[0], big_ref.shape[1]
    half = width // 2
    steps = big_ref.shape[0]
    big_ref[:, :half], big_ref[:, half:] = waves(steps, count, half)
    fine, middle = waves(16, 1, half), waves(count // 16, 16, half)
    for a in range(count // 16):
        at = slice(a * 16, (a + 1) * 16)
        row = [part[a : a + 1] for part in middle]
        for start, value in zip((0, half), turn(row, fine)):
            high, low = split(value)
            tab_ref[at, start : start + half] = high
            tab_ref[at, width + start : width + start + half] = low


def base_kernel(site_id_ref, probe_id_ref, site_ref, probe_ref, after_ref, base_ref):
    del after_ref
    sites, probes = site_ref.shape[0], probe_ref.shape[0]
    probe_id = probe_id_ref[...].reshape(1, 1)
    one_site = jnp.where(iota((16, sites), 1) == site_id_ref[...], 1.0, 0.0).astype(BF)
    one_probe = jnp.where(iota((16, probes), 1) == probe_id, 1.0, 0.0).astype(BF)
    base_ref[...] = mm(one_site, site_ref[...])[0:8] + mm(one_probe, probe_ref[...])[0:8]


def code_of(found, source, big_ref):
    width = big_ref.shape[1]
    half = width // 2
    local = found[:, :width] + found[:, width:]
    row = big_ref[pl.ds(source, 1), :]
    return jnp.concatenate(
        turn((row[:, :half], row[:, half:]), (local[:, :half], local[:, half:])), axis=1
    )


def own_kernel(
    keep_ref,
    volt_ref,
    token_ref,
    w_patch_ref,
    tab_ref,
    big_ref,
    base_ref,
    gain_ref,
    w_qkv_ref,
    after_ref,
    x0_ref,
    q_ref,
    self_ref,
    v_ref,
):
    del after_ref
    width = x0_ref.shape[1]
    code = code_of(tab_ref[...].astype(F32), lax.axis_index("tm"), big_ref)
    keep = to_column(keep_ref[...].astype(F32))
    proj = mm(volt_ref[...], w_patch_ref[...])
    proj = jnp.where(keep > 0.5, proj, vector(token_ref))
    x0 = (proj + base_ref[0:1, :] + code).astype(BF)
    x0_ref[...] = x0
    h1 = norm(x0.astype(F32), vector(gain_ref)).astype(BF)
    qkv = mm(h1, w_qkv_ref[...]).astype(BF)
    queries = (qkv[:, :width].astype(F32) * (1.0 / math.sqrt(HEAD_DIM))).astype(BF)
    q_ref[...] = queries
    v_ref[...] = qkv[:, 2 * width :]
    product = queries.astype(F32) * qkv[:, width : 2 * width].astype(F32)
    same_head = jnp.where(iota((128, 128), 0) // HEAD_DIM == iota((128, 128), 1) // HEAD_DIM, 1.0, 0.0).astype(BF)
    for pair in range(PAIRS):
        cols = slice(pair * 128, pair * 128 + 128)
        high, low = split(product[:, cols])
        score = mm(high, same_head) + mm(low, same_head)
        self_ref[:, cols] = jnp.where(keep > 0.5, FAR, score)


def keys_values(rows, offsets, cap, w_patch_ref, tab_ref, big_ref, base_ref, gain, w_qkv_ref):
    total = rows.shape[0]
    count, width = tab_ref.shape[0], base_ref.shape[1]
    samples = w_patch_ref.shape[0]
    local = rows[:, 384:512].astype(F32)[:, COL_TIME - 384 : COL_TIME - 383]
    proj = mm(rows[:, :samples], w_patch_ref[...])
    pick = jnp.where(iota((total, count), 1).astype(F32) == local, 1.0, 0.0).astype(BF)
    found = mm(pick, tab_ref[...])
    me = lax.axis_index("tm")
    x, z = me // NZ, lax.rem(me, NZ)
    code = []
    for i, (dx, dz) in enumerate(offsets):
        source = lax.rem(x + dx, NX) * NZ + lax.rem(z + dz + NZ, NZ)
        code.append(code_of(found[i * cap : (i + 1) * cap], source, big_ref))
    x0 = (proj + base_ref[0:1, :] + jnp.concatenate(code, axis=0)).astype(BF)
    h1 = norm(x0.astype(F32), gain).astype(BF)
    return mm(h1, w_qkv_ref[:, width:]).astype(BF)


def counts_of(rows, cap):
    heads = [rows[at : at + 1, COL_COUNT : COL_COUNT + 1] for at in range(0, rows.shape[0], cap)]
    return [head.astype(F32) for head in heads]


def cut(offsets, cap):
    each = max(1, 512 // cap)
    return [(at, offsets[at : at + each]) for at in range(0, len(offsets), each)]


def group_kernel(offsets, cap, nblocks, after, w_patch_ref, tab_ref, big_ref, base_ref, gain_ref, w_qkv_ref, *rest):
    blocks = rest[:nblocks]
    kv_ref, counts_ref = rest[nblocks + after :]
    rows = jnp.concatenate([block[...] for block in blocks], axis=0) if nblocks > 1 else blocks[0][...]
    for at, part in cut(offsets, cap):
        span = slice(at * cap, (at + len(part)) * cap)
        kv_ref[span, :] = keys_values(
            rows[span], part, cap, w_patch_ref, tab_ref, big_ref, base_ref, vector(gain_ref), w_qkv_ref
        )
    for i, number in enumerate(counts_of(rows, cap)):
        counts_ref[i : i + 1, :] = jnp.broadcast_to(number, (1, 128))


def both_heads(queries):
    low = iota(queries.shape, 1) < HEAD_DIM
    zero = jnp.zeros_like(queries)
    return jnp.concatenate([jnp.where(low, queries, zero), jnp.where(low, zero, queries)], axis=0)


def bias_of(counts, cap):
    place = iota((1, len(counts) * cap), 1)
    bias = jnp.full(place.shape, FAR, F32)
    for i, number in enumerate(counts):
        inside = (place >= i * cap) & ((place - i * cap).astype(F32) < jnp.minimum(number, cap))
        bias = jnp.where(inside, 0.0, bias)
    return bias


def score_kernel(cap, q_ref, *rest):
    groups, out_ref, top_ref = rest[:-2], rest[-2], rest[-1]
    groups, numbers = groups[::2], groups[1::2]
    bias = bias_of([ref[i : i + 1, 0:1] for ref in numbers for i in range(ref.shape[0])], cap)
    for pair in range(PAIRS):
        cols = slice(pair * 128, pair * 128 + 128)
        keys = jnp.concatenate([kv_ref[:, cols] for kv_ref in groups], axis=0)
        scores = lax.dot_general(both_heads(q_ref[:, cols]), keys, NT, preferred_element_type=F32) + bias
        out_ref[pair] = scores
        top_ref[pair] = jnp.broadcast_to(jnp.max(scores, axis=1, keepdims=True), top_ref.shape[1:])


def attend_kernel(
    offsets,
    cap,
    ngroups,
    nblocks,
    nearly,
    keep_ref,
    w_patch_ref,
    tab_ref,
    big_ref,
    base_ref,
    gain_ref,
    w_qkv_ref,
    q_ref,
    self_ref,
    v_ref,
    x0_ref,
    w_out_ref,
    *rest,
):
    groups, rest = rest[: 2 * ngroups], rest[2 * ngroups :]
    blocks, early = rest[:nblocks], rest[nblocks : nblocks + nearly]
    out_ref, kv, ctx = rest[nblocks + nearly :]
    count, width = x0_ref.shape
    rows = jnp.concatenate([block[...] for block in blocks], axis=0)
    counts, start = [], 0
    for kv_ref, counts_ref in zip(groups[::2], groups[1::2]):
        skip = width if early else 0
        kv[start : start + kv_ref.shape[0], skip:] = kv_ref[:, skip:]
        start += kv_ref.shape[0]
        counts += [counts_ref[i : i + 1, 0:1] for i in range(counts_ref.shape[0])]
    for at, part in cut(offsets, cap):
        kv[start + at * cap : start + (at + len(part)) * cap, :] = keys_values(
            rows[at * cap : (at + len(part)) * cap],
            part,
            cap,
            w_patch_ref,
            tab_ref,
            big_ref,
            base_ref,
            vector(gain_ref),
            w_qkv_ref,
        )
    counts += counts_of(rows, cap)
    keys = kv.shape[0]
    bias = bias_of(counts[start // cap :] if early else counts, cap)
    most = functools.reduce(jnp.maximum, counts)

    low = iota((count, 128), 1) < HEAD_DIM
    ones = jnp.ones((keys, 128), BF)

    def one_pair(pair):
        at = pair * 128 if isinstance(pair, int) else pl.multiple_of(pair * 128, 128)
        cols, value_cols = pl.ds(at, 128), pl.ds(width + at, 128)
        both = both_heads(q_ref[:, cols])
        keys_here = kv[start:, cols] if early else kv[:, cols]
        scores = lax.dot_general(both, keys_here, NT, preferred_element_type=F32) + bias
        top = jnp.max(scores, axis=1, keepdims=True)
        if early:
            scores = jnp.concatenate([early[0][pair], scores], axis=1)
            top = jnp.maximum(top, early[1][pair][:, 0:1])
        own = self_ref[:, cols]
        own = jnp.concatenate([own[:, 0:1], own[:, HEAD_DIM : HEAD_DIM + 1]], axis=0)
        top = jnp.maximum(top, own)
        weights = jnp.exp(scores - top).astype(BF)
        mixed = mm(weights, jnp.concatenate([kv[:, value_cols], ones], axis=1))
        own = jnp.exp(own - top)
        total = mixed[:, 128:] + own
        own = own.astype(BF).astype(F32)
        values = v_ref[:, cols].astype(F32)
        first = (mixed[:count, :128] + own[:count] * values) / total[:count]
        second = (mixed[count:, :128] + own[count:] * values) / total[count:]
        ctx[:, cols] = jnp.where(low, first, second).astype(BF)

    if keys <= 2048:
        for pair in range(PAIRS):
            one_pair(pair)
    else:
        pl.loop(0, PAIRS)(one_pair)
    x1 = x0_ref[...].astype(F32) + mm(ctx[...], w_out_ref[...])
    out_ref[:, :width] = x1.astype(BF)
    keep = to_column(keep_ref[...].astype(F32))
    over = jnp.where(most > cap, 1.0, 0.0)
    out_ref[:, width:] = jnp.where(iota((count, 128), 1) == 0, keep, over).astype(BF)


def cross_kernel(x_ref, gain_ref, w_qkv_ref, w_out_ref, out_ref, over_ref, ctx):
    count, width = out_ref.shape
    over_ref[0, 0] = jnp.max(x_ref[:, width:].astype(F32)[:, 1:2]).astype(jnp.int32)
    x1 = x_ref[:, :width].astype(F32)
    h2 = norm(x1, vector(gain_ref)).astype(BF)
    qkv = mm(h2, w_qkv_ref[...]).astype(BF)
    seen = x_ref[:, width:].astype(F32)[:, 0:1]
    eye = iota((count, count), 0) == iota((count, count), 1)
    seen = jnp.sum(jnp.where(eye, seen, 0.0), axis=0, keepdims=True)
    bias = jnp.where(eye | (seen > 0.5), 0.0, FAR)
    bias = jnp.concatenate([bias, bias], axis=0)
    lane = iota((count, 128), 1)
    low = lane < HEAD_DIM
    scale = 1.0 / math.sqrt(HEAD_DIM)
    ones = jnp.ones((count, 128), BF)
    for pair in range(PAIRS):
        at = pair * 128
        both = both_heads((qkv[:, at : at + 128].astype(F32) * scale).astype(BF))
        scores = lax.dot_general(both, qkv[:, width + at : width + at + 128], NT, preferred_element_type=F32)
        scores = scores + bias
        top = jnp.max(scores, axis=1, keepdims=True)
        weights = jnp.exp(scores - top).astype(BF)
        values = jnp.concatenate([qkv[:, 2 * width + at : 2 * width + at + 128], ones], axis=1)
        mixed = mm(weights, values)
        done = mixed[:, :128] / mixed[:, 128:]
        ctx[:, at : at + 128] = jnp.where(low, done[:count], done[count:]).astype(BF)
    out_ref[...] = (x1 + mm(ctx[...], w_out_ref[...])).astype(BF)


def body(
    volt,
    keep,
    site_ids,
    probe_ids,
    w_patch,
    site_table,
    probe_table,
    mask_token,
    gain_time,
    w_qkv_time,
    w_out_time,
    gain_cross,
    w_qkv_cross,
    w_out_cross,
):
    width = w_patch.shape[1]
    rows = volt[0, 0]
    count = rows.shape[0]
    mask = keep[0]
    steps = NX * NZ

    def shift(array, dx, dz):
        pairs = []
        for i in range(steps):
            x, z = divmod(i, NZ)
            pairs.append((i, ((x + dx) % NX) * NZ + (z + dz) % NZ))
        return lax.ppermute(array, "tm", pairs)

    def pack(cap):
        return call(
            pack_kernel,
            jax.ShapeDtypeStruct((cap, PACKED), BF),
            (mask, rows),
            scratch=(pltpu.VMEM((count, PACKED), BF),),
            vmem=4,
            flops=2 * cap * count * PACKED,
            nbytes=500_000,
        )

    packed = pack(CAP)
    tab, big = call(
        table_kernel,
        (jax.ShapeDtypeStruct((count, 2 * width), BF), jax.ShapeDtypeStruct((steps, width), F32)),
        (),
        vmem=8,
        flops=2_000_000_000,
        nbytes=1_000_000,
    )
    base = call(
        base_kernel,
        jax.ShapeDtypeStruct((8, width), F32),
        (site_ids, probe_ids, site_table, probe_table, big),
        vmem=4,
        flops=10_000_000,
        nbytes=200_000,
    )
    shared = (w_patch, tab, big, base, gain_time, w_qkv_time)

    def own_part(after):
        return call(
            own_kernel,
            (
                jax.ShapeDtypeStruct((count, width), BF),
                jax.ShapeDtypeStruct((count, width), BF),
                jax.ShapeDtypeStruct((count, width), F32),
                jax.ShapeDtypeStruct((count, width), BF),
            ),
            (mask, rows, mask_token, *shared, after),
            vmem=24,
            flops=300_000_000,
            nbytes=100_000,
        )

    def attend(own, cap, vmem, mine=None):
        def group(blocks, offsets, after=()):
            return call(
                functools.partial(group_kernel, offsets, cap, len(blocks), len(after)),
                (
                    jax.ShapeDtypeStruct((len(offsets) * cap, 2 * width), BF),
                    jax.ShapeDtypeStruct((len(offsets), 128), F32),
                ),
                (*shared, *blocks, *after),
                vmem=vmem,
                flops=2_500_000_000,
                nbytes=6_000_000,
            )

        below, above, beside = shift(own, 0, 1), shift(own, 0, -1), shift(own, 1, 0)
        first = group((own, below, above, beside), [(0, 0), (0, -1), (0, 1), (1, 0)])
        down2 = shift(jnp.concatenate([below, beside], axis=0), 0, 1)
        up2 = shift(jnp.concatenate([above, beside], axis=0), 0, -1)
        mine = mine or own_part(first[1])
        x0, queries, own_scores, own_values = mine
        second = group((down2, up2), [(0, -2), (1, -1), (0, 2), (1, 1)], (x0,))
        down3, up3 = shift(down2, 0, 1), shift(up2, 0, -1)
        third = group((down3, up3), [(0, -3), (1, -2), (0, 3), (1, 2)])
        down4 = shift(down3, 0, 1)
        far = shift(jnp.concatenate([up2[:cap], up3[:cap]], axis=0), 1, -1)
        early = ()
        if cap <= CAP:
            keys = sum(group[0].shape[0] for group in (first, second, third))
            early = call(
                functools.partial(score_kernel, cap),
                (
                    jax.ShapeDtypeStruct((PAIRS, 2 * count, keys), F32),
                    jax.ShapeDtypeStruct((PAIRS, 2 * count, 128), F32),
                ),
                (queries, *first, *second, *third),
                vmem=8,
                flops=300_000_000,
                nbytes=100_000,
            )
        last = [(0, -4), (1, -3), (1, 3), (1, 4)]
        return mine, call(
            functools.partial(attend_kernel, last, cap, 3, 2, len(early)),
            jax.ShapeDtypeStruct((count, width + 128), BF),
            (
                mask,
                *shared,
                queries,
                own_scores,
                own_values,
                x0,
                w_out_time,
                *first,
                *second,
                *third,
                down4,
                far,
                *early,
            ),
            scratch=(pltpu.VMEM((steps * cap, 2 * width), BF), pltpu.VMEM((count, width), BF)),
            vmem=vmem + 8,
            flops=12_000_000_000,
            nbytes=10_000_000,
        )

    def trade(array):
        return lax.all_to_all(array, ("probe", "lane"), split_axis=0, concat_axis=0, tiled=True)

    def cross(window):
        return call(
            cross_kernel,
            (jax.ShapeDtypeStruct((count, width), BF), jax.ShapeDtypeStruct((1, 1), jnp.int32)),
            (window, gain_cross, w_qkv_cross, w_out_cross),
            smem_out=(1,),
            scratch=(pltpu.VMEM((count, width), BF),),
            flops=2_000_000_000,
            nbytes=6_000_000,
        )

    mine, x1 = attend(packed, CAP, 20)
    done, over = cross(trade(x1))
    general = over[0, 0] > 0

    def trade_by_pairs(array):
        parts = count // WIN
        here = lax.axis_index("probe") * lax.axis_size("lane") + lax.axis_index("lane")
        out = array
        for k in range(1, parts):
            there = (here ^ k) * WIN
            part = lax.dynamic_slice_in_dim(array, there, WIN, 0)
            part = lax.ppermute(part, ("probe", "lane"), [(i, i ^ k) for i in range(parts)])
            out = lax.dynamic_update_slice_in_dim(out, part, there, 0)
        return out

    def again():
        return trade_by_pairs(cross(trade_by_pairs(attend(pack(count), count, 50, mine)[1]))[0])

    out = trade(done)
    out = jnp.where(general, lax.cond(general, again, lambda: jnp.zeros_like(done)), out)
    return out[None, None]


def solution(mesh):
    return jax.shard_map(
        body,
        mesh=mesh,
        in_specs=(
            P("probe", "lane", "tm", None),
            P("probe", "lane", "tm"),
            P("probe", "lane"),
            P("probe"),
            P(),
            P(),
            P(),
            P(),
            P(),
            P(),
            P(),
            P(),
            P(),
            P(),
        ),
        out_specs=P("probe", "lane", "tm", None),
        check_vma=False,
    )
```
